512 devices in a mesh: table: 32 (over x_lo, z, core), dp: 16 (over x_hi, y).
Axes of the slice: x: 4 (x_hi: 2, x_lo: 2; x = x_hi * 2 + x_lo), y: 8, z: 8, core: 2. Of those that a mesh axis runs over, the one named last changes fastest.
Arguments:
- ids: int32 [32, 8192, 128], P('table', 'dp'), may hold values from 0 to 1023
- mults: int32 [32, 8192, 128], P('table', 'dp'), may hold values from 0 to 2
- table: bfloat16 [32768, 128], P('table'), may hold values from -0.625 to 0.625
- user_layer: bfloat16 [1024, 512], replicated, may hold values from -0.1875 to 0.1875
- user_head: bfloat16 [512, 128], replicated, may hold values from -0.25 to 0.25
- item_layer: bfloat16 [1024, 512], replicated, may hold values from -0.1875 to 0.1875
- item_head: bfloat16 [512, 128], replicated, may hold values from -0.25 to 0.25
- counts: int32 [16, 512], P('dp', 'table'), may hold values from 1 to 256
Outputs:
- losses: float32 [16, 512], P('dp', 'table')
- table_change: float32 [32768, 128], P('table')
- user_layer_change: float32 [1024, 512], P('table')
- user_head_change: float32 [512, 128], P('table')
- item_layer_change: float32 [1024, 512], P('table')
- item_head_change: float32 [512, 128], P('table')
The draws below stay inside these ranges and needn't reach their ends.
All inputs are finite; a program needn't handle non-finite values.
Results may differ from the reference program's by a relative error of at most 0.039.
Values may be sent and summed in bfloat16 or wider, within the bound.
No kernel may reach another device: no remote copies, remote signals or barrier semaphores. Data moves between devices by JAX's collectives and lax.ppermute only.
A program may use at most 64 MiB of HBM per device.

```python
import jax
import jax.numpy as jnp
from jax import lax

EMB = 128
F_USER = 8
F_ITEM = 8
HID = 512
OUT = 128
LOOKUPS = 8
R_DEV = 1024
B_DEV = 16
BATCH = 8192
N_TABLE = 32
N_DP = 16


def plant(entries, rng, smallest, top_value):
    index_at = [jax.random.randint(jax.random.fold_in(rng, axis), (), 0, length) for axis, length in enumerate(entries.shape)]
    longest = entries.shape.index(max(entries.shape))
    beside = index_at[:longest] + [(index_at[longest] + 1) % entries.shape[longest]] + index_at[longest + 1:]
    return entries.at[tuple(index_at)].set(smallest).at[tuple(beside)].set(top_value)


def levels(rng, dims, cuts, low, high):
    gain = 1.0
    for axis_at, parts in cuts:
        heights = jax.random.uniform(jax.random.fold_in(jax.random.fold_in(rng, 6), axis_at), (parts,), jnp.float32, low / len(cuts), high / len(cuts))
        gain = gain * jnp.repeat(jnp.exp(heights), dims[axis_at] // parts).reshape((-1,) + (1,) * (len(dims) - 1 - axis_at))
    return gain


def noise(own_key, dims, deviation, limit, cuts=(), kind=jnp.bfloat16):
    entries = jax.random.normal(own_key, dims, jnp.float32) * deviation
    if len(cuts) > 0:
        entries = levels(own_key, dims, cuts, -0.22, 0.18) * entries
    return jnp.clip(entries, min=-limit, max=limit).astype(kind)


def setup_inputs(seed: int = 0) -> dict:
    key_of = jax.random.split(jax.random.key(seed), 9)
    ids = plant(jax.random.randint(key_of[0], (N_TABLE, BATCH, (F_USER + F_ITEM) * LOOKUPS), 0, R_DEV), jax.random.fold_in(key_of[0], 1), 0, R_DEV - 1).astype(jnp.int32)
    mults = plant(jax.random.randint(key_of[1], (N_TABLE, BATCH, (F_USER + F_ITEM) * LOOKUPS), 0, 3), jax.random.fold_in(key_of[1], 1), 0, 2).astype(jnp.int32)
    table = noise(key_of[2], (N_TABLE * R_DEV, EMB), ((2 * N_TABLE * LOOKUPS) ** -0.5), 0.625, ((0, 32),))
    user_layer = noise(key_of[3], (F_USER * EMB, HID), (F_USER * EMB) ** -0.5, 0.1875)
    user_head = noise(key_of[4], (HID, OUT), HID ** -0.5, 0.25)
    item_layer = noise(key_of[5], (F_ITEM * EMB, HID), (F_ITEM * EMB) ** -0.5, 0.1875)
    item_head = noise(key_of[6], (HID, OUT), HID ** -0.5, 0.25)
    counts = plant(jax.random.randint(key_of[7], (N_DP, N_TABLE * B_DEV), 1, 257), jax.random.fold_in(key_of[7], 1), 1, 256).astype(jnp.int32)
    return {"ids": ids, "mults": mults, "table": table, "user_layer": user_layer, "user_head": user_head, "item_layer": item_layer, "item_head": item_head, "counts": counts}


INVERSE_TEMP = 20.0
EPSILON = 1e-06

def silu_slope(pre):
    gate = jax.nn.sigmoid(pre)
    return gate * (1.0 + pre * (1.0 - gate))

def run_tower(pooled_in, layer, head):
    pre = jnp.dot(pooled_in, layer, preferred_element_type=jnp.float32)
    hidden = jax.nn.silu(pre).astype(jnp.bfloat16)
    output = jnp.dot(hidden, head, preferred_element_type=jnp.float32)
    return (pre, hidden, output)

def unit_scale(output):
    return lax.rsqrt(lax.optimization_barrier(jnp.sum(output * output, axis=-1, keepdims=True)) + EPSILON)

def tower_back(d_unit, output, pre, layer, head):
    scale = unit_scale(output)
    unit = output * scale
    along = lax.optimization_barrier(jnp.sum(unit * d_unit, axis=-1, keepdims=True))
    d_output = ((d_unit - unit * along) * scale).astype(jnp.bfloat16)
    d_hidden = (jnp.dot(d_output, head.T, preferred_element_type=jnp.float32) * silu_slope(pre)).astype(jnp.bfloat16)
    d_pooled = jnp.dot(d_hidden, layer.T, preferred_element_type=jnp.float32).astype(jnp.bfloat16)
    return (d_output, d_hidden, d_pooled)

def rounded_term(left, right):
    term = jnp.dot(left.T, right, preferred_element_type=jnp.float32).astype(jnp.bfloat16)
    return lax.optimization_barrier(term).astype(jnp.float32)

def reference(ids, mults, table, user_layer, user_head, item_layer, item_head, counts):
    feature_count = F_USER + F_ITEM
    group_rows = B_DEV * N_TABLE
    batch_rows = group_rows * N_DP
    shard_list = jnp.arange(N_TABLE, dtype=jnp.int32)

    def shard_inputs(shard):
        shard_ids = lax.dynamic_index_in_dim(ids, shard, 0, keepdims=False)
        shard_mults = lax.dynamic_index_in_dim(mults, shard, 0, keepdims=False)
        shape = (N_DP, group_rows, feature_count, LOOKUPS)
        return (shard_ids.reshape(shape).astype(jnp.int32), shard_mults.reshape(shape))

    def shard_pool(running, shard):
        rows = lax.dynamic_slice_in_dim(table, shard * R_DEV, R_DEV, 0).astype(jnp.float32)
        shard_ids, shard_mults = shard_inputs(shard)

        def block_pool(lookup_pair):
            picked = rows[lookup_pair[0]]
            return lax.optimization_barrier(jnp.sum(picked * lookup_pair[1].astype(jnp.float32)[..., None], axis=2)).astype(jnp.bfloat16)
        partial_value = lax.map(block_pool, (shard_ids, shard_mults))
        return (running + partial_value.astype(jnp.float32), None)
    summed, _ = lax.scan(shard_pool, jnp.zeros((N_DP, group_rows, feature_count, EMB), jnp.float32), shard_list)
    pooled = summed.astype(jnp.bfloat16).reshape(batch_rows, feature_count * EMB)
    user_width = F_USER * EMB
    user_in = pooled[:, :user_width]
    item_in = pooled[:, user_width:]
    user_pre, user_hidden, user_output = run_tower(user_in, user_layer, user_head)
    item_pre, item_hidden, item_output = run_tower(item_in, item_layer, item_head)
    user_unit = (user_output * unit_scale(user_output)).astype(jnp.bfloat16)
    item_unit = (item_output * unit_scale(item_output)).astype(jnp.bfloat16)

    def by_table(values):
        return values.reshape(N_DP, N_TABLE, B_DEV, -1).transpose(1, 0, 2, 3).reshape(N_TABLE, N_DP * B_DEV, -1)

    def by_batch(values):
        return values.reshape(N_TABLE, N_DP, B_DEV, -1).transpose(1, 0, 2, 3).reshape(batch_rows, -1)
    queries = by_table(user_unit).astype(jnp.float32)
    keys = by_table(item_unit).astype(jnp.float32)
    log_freq = by_table(jnp.log(counts.astype(jnp.float32)).reshape(batch_rows, 1))[..., 0]
    scores = INVERSE_TEMP * jnp.einsum('tik,tjk->tij', queries, keys) - log_freq[:, None, :]
    lse = jnp.log(lax.optimization_barrier(jnp.sum(jnp.exp(scores), axis=-1)))
    identity = jnp.eye(N_DP * B_DEV, dtype=jnp.float32)
    positive = lax.optimization_barrier(jnp.sum(scores * identity, axis=-1))
    losses = by_batch((lse - positive)[..., None]).reshape(N_DP, N_TABLE * B_DEV)
    dscore = (jnp.exp(scores - lse[..., None]) - identity).astype(jnp.bfloat16)
    dscore = lax.optimization_barrier(dscore).astype(jnp.float32)
    d_query = INVERSE_TEMP * jnp.einsum('tij,tjk->tik', dscore, keys)
    d_key = INVERSE_TEMP * jnp.einsum('tij,tik->tjk', dscore, queries)
    user_dout, user_dhid, user_dpool = tower_back(by_batch(d_query), user_output, user_pre, user_layer, user_head)
    item_dout, item_dhid, item_dpool = tower_back(by_batch(d_key), item_output, item_pre, item_layer, item_head)
    device_count = N_DP * N_TABLE

    def per_device(values):
        return values.reshape(device_count, B_DEV, values.shape[-1])

    def add_device(running, blocks):
        u_in, u_hid, u_dout, u_dhid, i_in, i_hid, i_dout, i_dhid = blocks
        terms = (rounded_term(u_in, u_dhid), rounded_term(u_hid, u_dout), rounded_term(i_in, i_dhid), rounded_term(i_hid, i_dout))
        return (tuple((a + b for a, b in zip(running, terms))), None)
    starts = (jnp.zeros(user_layer.shape, jnp.float32), jnp.zeros(user_head.shape, jnp.float32), jnp.zeros(item_layer.shape, jnp.float32), jnp.zeros(item_head.shape, jnp.float32))
    blocks = tuple((per_device(v) for v in (user_in, user_hidden, user_dout, user_dhid, item_in, item_hidden, item_dout, item_dhid)))
    changes, _ = lax.scan(add_device, starts, blocks)
    d_pooled = jnp.concatenate([user_dpool, item_dpool], axis=1).reshape(N_DP, group_rows, feature_count, EMB)

    def shard_grad(shard):
        shard_ids, shard_mults = shard_inputs(shard)

        def block_grad(triple):
            values = triple[2].astype(jnp.float32)[:, :, None, :] * triple[1].astype(jnp.float32)[..., None]
            return jax.ops.segment_sum(values.reshape(-1, EMB), triple[0].reshape(-1), num_segments=R_DEV)
        return lax.optimization_barrier(jnp.sum(lax.map(block_grad, (shard_ids, shard_mults, d_pooled)), axis=0))
    table_change = lax.map(shard_grad, shard_list).reshape(N_TABLE * R_DEV, EMB)
    return (losses, table_change, changes[0], changes[1], changes[2], changes[3])
```

```python
import jax
import jax.numpy as jnp
from jax import lax
from jax.experimental import pallas as pl
from jax.experimental.pallas import tpu as pltpu
from jax.sharding import Mesh
from jax.sharding import PartitionSpec as P

LOOKUPS = 8
INVERSE_TEMP = 20.0
EPSILON = 1e-06

AXES = {"x_lo": 2, "z": 8, "core": 2, "x_hi": 2, "y": 8}
TABLE = ("x_lo", "z", "core")
CHIPS = ("x_lo", "z")
DP = ("x_hi", "y")
N_CHIP = 16
N_DP = 16
OWN = 16
FEATURES = 16
TOWER_FEATURES = 8
ROWS = 1024
EMB = 128
HID = 512
OUT = 128
BLOCK = OWN * FEATURES
IN_WIDTH = TOWER_FEATURES * EMB
GRAD_WIDTH = 12 * 128
COLUMNS_AT = 2 * HID + 2 * OUT
CHUNK = 96

BF16 = jnp.bfloat16
F32 = jnp.float32
PARAMS = pltpu.CompilerParams(vmem_limit_bytes=56 * 1024 * 1024)

NT = (((1,), (1,)), ((), ()))
TN = (((0,), (0,)), ((), ()))


def dot(left, right, dims=(((1,), (0,)), ((), ()))):
    return lax.dot_general(left, right, dims, preferred_element_type=F32)


def whole():
    return pl.BlockSpec(memory_space=pltpu.VMEM)


def pool_kernel(core_ref, ids_ref, mults_ref, table_ref, weights_ref, partial_ref):
    ids = ids_ref[...]
    lane = lax.broadcasted_iota(jnp.int32, ids.shape, 1)
    high = lax.shift_right_logical(ids, 7) * FEATURES + lax.shift_right_logical(lane, 3)
    high = high.astype(F32)
    low = (ids & 127).astype(F32)
    mults = mults_ref[...].astype(F32)
    row = lax.broadcasted_iota(jnp.int32, (128, 128), 0).astype(F32)
    zero = jnp.zeros((128, 128), F32)
    one = jnp.ones((128, 128), F32)
    for n in range(OWN):
        left = jnp.where(high[n : n + 1] == row, mults[n : n + 1], zero).astype(BF16)
        right = jnp.where(low[n : n + 1] == row, one, zero).astype(BF16)
        hits = dot(left, right, NT).astype(BF16)
        for h in range(8):
            weights_ref[n * FEATURES : (n + 1) * FEATURES, h * 128 : (h + 1) * 128] = hits[
                h * FEATURES : (h + 1) * FEATURES
            ]
    partial_ref[...] = dot(weights_ref[...], table_ref[...]).astype(BF16)


def pool(core, ids, mults, table):
    def picked(i, core_ref):
        return (2 * i + core_ref[0], 0)

    def at(i, core_ref):
        return (i, 0)

    return pl.pallas_call(
        pool_kernel,
        grid_spec=pltpu.PrefetchScalarGridSpec(
            num_scalar_prefetch=1,
            grid=(N_CHIP,),
            in_specs=[
                pl.BlockSpec((OWN, 128), picked),
                pl.BlockSpec((OWN, 128), picked),
                pl.BlockSpec((ROWS, EMB), lambda i, core_ref: (0, 0)),
            ],
            out_specs=[pl.BlockSpec((BLOCK, ROWS), at), pl.BlockSpec((BLOCK, EMB), at)],
        ),
        out_shape=[
            jax.ShapeDtypeStruct((N_CHIP * BLOCK, ROWS), BF16),
            jax.ShapeDtypeStruct((N_CHIP * BLOCK, EMB), BF16),
        ],
        compiler_params=PARAMS,
        cost_estimate=pl.CostEstimate(
            flops=2 * N_CHIP * BLOCK * ROWS * EMB * 2, bytes_accessed=10 * 2**20, transcendentals=0
        ),
        name="pool",
    )(core, ids, mults, table)


def column_of(row):
    eye = lax.broadcasted_iota(jnp.int32, (OWN, OWN), 0) == lax.broadcasted_iota(
        jnp.int32, (OWN, OWN), 1
    )
    return jnp.sum(jnp.where(eye, row, 0.0), axis=1, keepdims=True)


def row_of(column):
    eye = lax.broadcasted_iota(jnp.int32, (OWN, OWN), 0) == lax.broadcasted_iota(
        jnp.int32, (OWN, OWN), 1
    )
    return jnp.sum(jnp.where(eye, column, 0.0), axis=0, keepdims=True)


def tower_kernel(
    parts_ref, counts_ref, layer0_ref, head0_ref, layer1_ref, head1_ref,
    pooled_ref, pre_ref, hidden_ref, unit_ref, scale_ref, send_ref, rows_ref,
):
    total = parts_ref[0].astype(F32)
    for s in range(1, N_CHIP):
        total = total + parts_ref[s].astype(F32)
    rows_ref[...] = total
    for f in range(FEATURES):
        pooled_ref[:, f * EMB : (f + 1) * EMB] = rows_ref[
            pl.ds(f, OWN, stride=FEATURES), :
        ].astype(BF16)
    for tower, (layer_ref, head_ref) in enumerate(((layer0_ref, head0_ref), (layer1_ref, head1_ref))):
        pooled = pooled_ref[:, tower * IN_WIDTH : (tower + 1) * IN_WIDTH]
        pre = dot(pooled, layer_ref[...])
        hidden = (pre * (1.0 / (1.0 + jnp.exp(-pre)))).astype(BF16)
        output = dot(hidden, head_ref[...])
        scale = lax.rsqrt(jnp.sum(output * output, axis=-1, keepdims=True) + EPSILON)
        unit = output * scale
        pre_ref[:, tower * HID : (tower + 1) * HID] = pre
        hidden_ref[:, tower * HID : (tower + 1) * HID] = hidden
        unit_ref[:, tower * OUT : (tower + 1) * OUT] = unit
        scale_ref[:, tower * OUT : (tower + 1) * OUT] = jnp.broadcast_to(scale, (OWN, OUT))
        rounded = unit.astype(BF16)
        for d in range(N_DP):
            send_ref[d, tower * OWN : (tower + 1) * OWN, :] = rounded
    counts = column_of(counts_ref[...].astype(F32))
    spread = jnp.broadcast_to(counts, (OWN, 128)).astype(BF16)
    for d in range(N_DP):
        send_ref[d, 2 * OWN : 3 * OWN, :] = spread


def towers(parts, counts, layer0, head0, layer1, head1):
    return pl.pallas_call(
        tower_kernel,
        in_specs=[whole()] * 6,
        out_specs=[whole()] * 6,
        out_shape=[
            jax.ShapeDtypeStruct((OWN, FEATURES * EMB), BF16),
            jax.ShapeDtypeStruct((OWN, 2 * HID), F32),
            jax.ShapeDtypeStruct((OWN, 2 * HID), BF16),
            jax.ShapeDtypeStruct((OWN, 2 * OUT), F32),
            jax.ShapeDtypeStruct((OWN, 2 * OUT), F32),
            jax.ShapeDtypeStruct((N_DP, 3 * OWN, 128), BF16),
        ],
        scratch_shapes=[pltpu.VMEM((BLOCK, EMB), F32)],
        compiler_params=PARAMS,
        name="towers",
    )(parts, counts, layer0, head0, layer1, head1)


def softmax_kernel(
    place_ref, group_ref, counts_ref, pooled_ref, pre_ref, hidden_ref, unit_ref, scale_ref,
    head0_ref, head1_ref, losses_ref, send_ref,
):
    size = N_DP * OWN
    group = group_ref[...]
    users = group[:, :OWN].reshape(size, OUT)
    items = group[:, OWN : 2 * OWN].reshape(size, OUT)
    log_freq = jnp.log(group[:, 2 * OWN :].reshape(size, 128).astype(F32))
    log_row = jnp.transpose(log_freq)[:1]
    own_log = jnp.log(column_of(counts_ref[...].astype(F32)))
    own_user = unit_ref[:, :OUT].astype(BF16)
    own_item = unit_ref[:, OUT:].astype(BF16)
    first = place_ref[0] * OWN
    mine = lax.broadcasted_iota(jnp.int32, (OWN, size), 1) == (
        lax.broadcasted_iota(jnp.int32, (OWN, size), 0) + first
    )
    down = INVERSE_TEMP * dot(items, users, NT) - jnp.concatenate([log_freq, log_freq], axis=1)
    lse_row = jnp.log(jnp.sum(jnp.exp(down), axis=0, keepdims=True))
    scores = INVERSE_TEMP * dot(own_user, items, NT) - log_row
    lse = jnp.log(jnp.sum(jnp.exp(scores), axis=1, keepdims=True))
    positive = jnp.sum(jnp.where(mine, scores, 0.0), axis=1, keepdims=True)
    losses_ref[...] = row_of(lse - positive)
    hot = mine.astype(F32)
    d_user = INVERSE_TEMP * dot((jnp.exp(scores - lse) - hot).astype(BF16), items)
    own_down = INVERSE_TEMP * dot(own_item, users, NT) - own_log
    d_item = INVERSE_TEMP * dot((jnp.exp(own_down - lse_row) - hot).astype(BF16), users)
    common = []
    outputs = []
    for tower, (d_unit, head_ref) in enumerate(((d_user, head0_ref), (d_item, head1_ref))):
        unit = unit_ref[:, tower * OUT : (tower + 1) * OUT]
        scale = scale_ref[:, tower * OUT : (tower + 1) * OUT]
        along = jnp.sum(unit * d_unit, axis=-1, keepdims=True)
        d_output = ((d_unit - unit * along) * scale).astype(BF16)
        pre = pre_ref[:, tower * HID : (tower + 1) * HID]
        gate = 1.0 / (1.0 + jnp.exp(-pre))
        slope = gate * (1.0 + pre * (1.0 - gate))
        common.append((dot(d_output, head_ref[...], NT) * slope).astype(BF16))
        outputs.append(d_output)
    common = jnp.concatenate(common + outputs, axis=1)
    pooled = pooled_ref[...]
    hidden = hidden_ref[...]
    blank = jnp.zeros((OWN, 64), BF16)
    for chip in range(N_CHIP):
        send_ref[chip, :, :COLUMNS_AT] = common
        send_ref[chip, :, COLUMNS_AT:] = jnp.concatenate(
            [
                pooled[:, chip * 64 : chip * 64 + 64],
                pooled[:, IN_WIDTH + chip * 64 : IN_WIDTH + chip * 64 + 64],
                hidden[:, chip * 32 : chip * 32 + 32],
                hidden[:, HID + chip * 32 : HID + chip * 32 + 32],
                blank,
            ],
            axis=1,
        )


def softmax_back(place, group, counts, pooled, pre, hidden, unit, scale, head0, head1):
    return pl.pallas_call(
        softmax_kernel,
        in_specs=[pl.BlockSpec(memory_space=pltpu.SMEM)] + [whole()] * 9,
        out_specs=[whole()] * 2,
        out_shape=[
            jax.ShapeDtypeStruct((1, OWN), F32),
            jax.ShapeDtypeStruct((N_CHIP, OWN, GRAD_WIDTH), BF16),
        ],
        compiler_params=PARAMS,
        name="softmax_back",
    )(place, group, counts, pooled, pre, hidden, unit, scale, head0, head1)


def back_kernel(first, last, *refs):
    if first:
        core_ref, grads_ref, weights_ref, layer0_ref, layer1_ref = refs[:5]
        refs = refs[5:]
    else:
        (core_ref, grads_ref, weights_ref, layer0_ref, layer1_ref, before_ref, layers_before_ref,
         heads_before_ref) = refs[:8]
        refs = refs[8:]
    if last:
        send_ref, total_ref, pooled_ref, layers_ref, heads_ref = refs
    else:
        total_ref, layers_ref, heads_ref, pooled_ref = refs
    step = pl.program_id(0)
    samples = N_CHIP * OWN

    @pl.when(step == 0)
    def _():
        grads = grads_ref[...].reshape(samples, GRAD_WIDTH)
        inputs = grads[:, COLUMNS_AT : COLUMNS_AT + 128]
        hidden = grads[:, COLUMNS_AT + 128 :]
        d_hidden = (grads[:, :HID], grads[:, HID : 2 * HID])
        for f in range(FEATURES):
            tower = f // TOWER_FEATURES
            layer_ref = (layer0_ref, layer1_ref)[tower]
            at = (f % TOWER_FEATURES) * EMB
            pooled_ref[pl.ds(f, samples, stride=FEATURES), :] = dot(
                d_hidden[tower], layer_ref[at : at + EMB, :], NT
            )
        for tower in range(2):
            d_output = grads[:, 2 * HID + tower * OUT : 2 * HID + (tower + 1) * OUT]
            layer_rows = dot(inputs, d_hidden[tower], TN)[tower * 64 : tower * 64 + 64]
            head_rows = dot(hidden, d_output, TN)[tower * 32 : tower * 32 + 32]
            if not first:
                layer_rows = layer_rows + layers_before_ref[tower]
                head_rows = head_rows + heads_before_ref[tower]
            layers_ref[tower] = layer_rows
            heads_ref[tower] = head_rows

    d_pooled = pooled_ref[pl.ds(pl.multiple_of(step * BLOCK, BLOCK), BLOCK), :].astype(BF16)
    term = dot(d_pooled, weights_ref[...], TN)

    @pl.when(step == 0)
    def _():
        total_ref[...] = term if first else before_ref[...] + term

    @pl.when(step > 0)
    def _():
        total_ref[...] += term

    if last:

        @pl.when(step == N_CHIP - 1)
        def _():
            table_rows = jnp.transpose(total_ref[...])
            core = core_ref[0]
            for d in range(N_DP):
                send_ref[d, :64, :] = table_rows[d * 64 : (d + 1) * 64].astype(BF16)
                tower, quarter, half = d // 8, d % 8 // 2, d % 2
                send_ref[d, 64:80, :] = layers_ref[
                    tower,
                    pl.ds(pl.multiple_of(core * 32 + half * 16, 16), 16),
                    quarter * 128 : quarter * 128 + 128,
                ].astype(BF16)
                if d < 2:
                    send_ref[d, 80:, :] = heads_ref[
                        d, pl.ds(pl.multiple_of(core * 16, 16), 16), :
                    ].astype(BF16)
                else:
                    send_ref[d, 80:, :] = jnp.zeros((16, 128), BF16)


def back(core, grads, weights, layer0, layer1, before=None):
    first = last = False
    if before is None:
        first = True
    else:
        last = True

    def fixed(shape):
        return pl.BlockSpec(shape, lambda i: (0,) * len(shape))

    total = jax.ShapeDtypeStruct((EMB, ROWS), F32)
    layers = jax.ShapeDtypeStruct((2, 64, HID), F32)
    heads = jax.ShapeDtypeStruct((2, 32, OUT), F32)
    pooled = pltpu.VMEM((N_CHIP * BLOCK, EMB), F32)
    in_specs = [
        pl.BlockSpec(memory_space=pltpu.SMEM),
        fixed((N_CHIP, OWN, GRAD_WIDTH)),
        pl.BlockSpec((BLOCK, ROWS), lambda i: (i, 0)),
        fixed((IN_WIDTH, HID)),
        fixed((IN_WIDTH, HID)),
    ]
    if last:
        in_specs += [fixed(total.shape), fixed(layers.shape), fixed(heads.shape)]
        out_shape = [jax.ShapeDtypeStruct((N_DP, CHUNK, 128), BF16)]
        scratch = [pltpu.VMEM(total.shape, F32), pooled, pltpu.VMEM(layers.shape, F32), pltpu.VMEM(heads.shape, F32)]
    else:
        out_shape = [total, layers, heads]
        scratch = [pooled]
    return pl.pallas_call(
        lambda *refs: back_kernel(first, last, *refs),
        grid=(N_CHIP,),
        in_specs=in_specs,
        out_specs=[fixed(s.shape) for s in out_shape],
        out_shape=out_shape,
        scratch_shapes=scratch,
        compiler_params=PARAMS,
        cost_estimate=pl.CostEstimate(
            flops=2 * N_CHIP * BLOCK * ROWS * EMB, bytes_accessed=10 * 2**20, transcendentals=0
        ),
        name="back",
    )(core, grads, weights, layer0, layer1, *(before or ()))


def sum_kernel(parts_ref, send_ref):
    total = parts_ref[0].astype(F32)
    for d in range(1, N_DP):
        total = total + parts_ref[d].astype(F32)
    total = total.astype(BF16)
    for d in range(N_DP):
        send_ref[d] = total


def sum_parts(parts):
    return pl.pallas_call(
        sum_kernel,
        in_specs=[whole()],
        out_specs=whole(),
        out_shape=jax.ShapeDtypeStruct(parts.shape, BF16),
        compiler_params=PARAMS,
        name="sum_parts",
    )(parts)


def spread_kernel(sums_ref, table_ref, layer0_ref, head0_ref, layer1_ref, head1_ref):
    for d in range(N_DP):
        table_ref[d * 64 : (d + 1) * 64, :] = sums_ref[d, :64, :].astype(F32)
        tower, quarter, half = d // 8, d % 8 // 2, d % 2
        (layer0_ref, layer1_ref)[tower][
            half * 16 : half * 16 + 16, quarter * 128 : quarter * 128 + 128
        ] = sums_ref[d, 64:80, :].astype(F32)
    head0_ref[...] = sums_ref[0, 80:, :].astype(F32)
    head1_ref[...] = sums_ref[1, 80:, :].astype(F32)


def spread(sums):
    return pl.pallas_call(
        spread_kernel,
        in_specs=[whole()],
        out_specs=[whole()] * 5,
        out_shape=[
            jax.ShapeDtypeStruct((ROWS, EMB), F32),
            jax.ShapeDtypeStruct((32, HID), F32),
            jax.ShapeDtypeStruct((16, OUT), F32),
            jax.ShapeDtypeStruct((32, HID), F32),
            jax.ShapeDtypeStruct((16, OUT), F32),
        ],
        compiler_params=PARAMS,
        name="spread",
    )(sums)


def exchange(values, axes):
    return lax.all_to_all(values, axes, 0, 0, tiled=True)


def to_other_core(values):
    return lax.ppermute(values, "core", [(0, 1), (1, 0)])


def shards(ids, mults, table, user_layer, user_head, item_layer, item_head, counts):
    core = lax.axis_index("core").reshape(1)
    place = lax.axis_index(DP).reshape(1)
    other_weights, other_partial = pool(1 - core, ids[0], mults[0], table)
    arrived = to_other_core(other_partial)
    own_weights, own_partial = pool(core, ids[0], mults[0], table)
    chip_partial = (own_partial.astype(F32) + arrived.astype(F32)).astype(BF16)
    parts = exchange(chip_partial.reshape(N_CHIP, BLOCK, EMB), CHIPS)
    pooled, pre, hidden, unit, scale, units = towers(
        parts, counts, user_layer, user_head, item_layer, item_head
    )
    group = exchange(units, DP)
    losses, grads = softmax_back(
        place, group, counts, pooled, pre, hidden, unit, scale, user_head, item_head
    )
    own_grads = exchange(grads, CHIPS)
    other_grads = to_other_core(own_grads)
    before = back(core, own_grads, own_weights, user_layer, item_layer)
    (terms,) = back(core, other_grads, other_weights, user_layer, item_layer, tuple(before))
    sums = exchange(sum_parts(exchange(terms, DP)), DP)
    table_change, layer0, head0, layer1, head1 = spread(sums)
    return (losses, table_change, layer0, head0, layer1, head1)


def solution(mesh):
    fine = Mesh(mesh.devices.reshape(tuple(AXES.values())), tuple(AXES))
    in_specs = (
        P(TABLE, DP, None),
        P(TABLE, DP, None),
        P(TABLE, None),
        P(),
        P(),
        P(),
        P(),
        P(DP, TABLE),
    )
    out_specs = (P(DP, TABLE),) + (P(TABLE, None),) * 5
    return jax.shard_map(shards, mesh=fine, in_specs=in_specs, out_specs=out_specs, check_vma=False)
```

```python
import jax
import jax.numpy as jnp
from jax import lax
from jax.experimental import pallas as pl
from jax.experimental.pallas import tpu as pltpu
from jax.sharding import Mesh
from jax.sharding import PartitionSpec as P

LOOKUPS = 8
INVERSE_TEMP = 20.0
EPSILON = 1e-06

AXES = {"x_lo": 2, "z": 8, "core": 2, "x_hi": 2, "y": 8}
TABLE = ("x_lo", "z", "core")
CHIPS = ("x_lo", "z")
DP = ("x_hi", "y")
N_CHIP = 16
N_DP = 16
OWN = 16
FEATURES = 16
TOWER_FEATURES = 8
ROWS = 1024
EMB = 128
HID = 512
OUT = 128
BLOCK = OWN * FEATURES
IN_WIDTH = TOWER_FEATURES * EMB
GRAD_WIDTH = 12 * 128
COLUMNS_AT = 2 * HID + 2 * OUT
POOL_SAMPLES = 64
BACK_PARTS = 4
CHUNK = 96

BF16 = jnp.bfloat16
F32 = jnp.float32
PARAMS = pltpu.CompilerParams(vmem_limit_bytes=56 * 1024 * 1024)

NT = (((1,), (1,)), ((), ()))
TN = (((0,), (0,)), ((), ()))


def dot(left, right, dims=(((1,), (0,)), ((), ()))):
    return lax.dot_general(left, right, dims, preferred_element_type=F32)


def whole():
    return pl.BlockSpec(memory_space=pltpu.VMEM)


def lookup_weights(ids, mults, weights_ref, first):
    lane = lax.broadcasted_iota(jnp.int32, ids.shape, 1)
    high = lax.shift_right_logical(ids, 7) * FEATURES + lax.shift_right_logical(lane, 3)
    high = high.astype(F32)
    low = jnp.transpose((ids & 127).astype(F32))
    mults = mults.astype(F32)
    down = lax.broadcasted_iota(jnp.int32, (128, 128), 0).astype(F32).astype(BF16)
    across = lax.broadcasted_iota(jnp.int32, (128, 128), 1).astype(F32).astype(BF16)
    zero = jnp.zeros((128, 128), BF16)
    one = jnp.ones((128, 128), BF16)

    def spread_row(values, n):
        row = jnp.broadcast_to(values[n : n + 1], (16, 128)).astype(BF16)
        return jnp.concatenate([row] * 8, axis=0)

    for n in range(ids.shape[0]):
        left = jnp.where(spread_row(high, n) == down, spread_row(mults, n), zero)
        spread_low = jnp.broadcast_to(low[:, n : n + 1], (128, 128)).astype(BF16)
        right = jnp.where(spread_low == across, one, zero)
        hits = dot(left, right).astype(BF16)
        at = first + n * FEATURES
        for h in range(8):
            weights_ref[at : at + FEATURES, h * 128 : (h + 1) * 128] = hits[
                h * FEATURES : (h + 1) * FEATURES
            ]


def pool_kernel(ids_ref, mults_ref, table_ref, out_ref, partial_ref, weights_ref, sems):
    parts = N_CHIP * OWN // POOL_SAMPLES
    rows = POOL_SAMPLES * FEATURES

    def copy(part):
        at = pl.ds(part * rows, rows)
        return pltpu.make_async_copy(weights_ref.at[at, :], out_ref.at[at, :], sems.at[part])

    def sum_part(part):
        at = pl.ds(part * rows, rows)
        partial_ref[at, :] = dot(weights_ref[at, :], table_ref[...]).astype(BF16)

    for part in range(parts):
        at = pl.ds(part * POOL_SAMPLES, POOL_SAMPLES)
        lookup_weights(ids_ref[at, :], mults_ref[at, :], weights_ref, part * rows)
        copy(part).start()
        if part > 0:
            sum_part(part - 1)
    sum_part(parts - 1)
    for part in range(parts):
        copy(part).wait()


def pool(ids, mults, table):
    parts = N_CHIP * OWN // POOL_SAMPLES
    return pl.pallas_call(
        pool_kernel,
        in_specs=[whole()] * 3,
        out_specs=[pl.BlockSpec(memory_space=pl.ANY), whole()],
        out_shape=[
            jax.ShapeDtypeStruct((N_CHIP * BLOCK, ROWS), BF16),
            jax.ShapeDtypeStruct((N_CHIP * BLOCK, EMB), BF16),
        ],
        scratch_shapes=[
            pltpu.VMEM((N_CHIP * BLOCK, ROWS), BF16),
            pltpu.SemaphoreType.DMA((parts,)),
        ],
        compiler_params=PARAMS,
        cost_estimate=pl.CostEstimate(
            flops=2 * N_CHIP * BLOCK * ROWS * EMB * 2, bytes_accessed=10 * 2**20, transcendentals=0
        ),
        name="pool",
    )(ids, mults, table)


def column_of(row):
    eye = lax.broadcasted_iota(jnp.int32, (OWN, OWN), 0) == lax.broadcasted_iota(
        jnp.int32, (OWN, OWN), 1
    )
    return jnp.sum(jnp.where(eye, row, 0.0), axis=1, keepdims=True)


def row_of(column):
    eye = lax.broadcasted_iota(jnp.int32, (OWN, OWN), 0) == lax.broadcasted_iota(
        jnp.int32, (OWN, OWN), 1
    )
    return jnp.sum(jnp.where(eye, column, 0.0), axis=0, keepdims=True)


def tower_kernel(
    parts_ref, counts_ref, layer0_ref, head0_ref, layer1_ref, head1_ref,
    pooled_ref, pre_ref, hidden_ref, unit_ref, scale_ref, send_ref, rows_ref,
):
    total = parts_ref[0].astype(F32)
    for s in range(1, N_CHIP):
        total = total + parts_ref[s].astype(F32)
    rows_ref[...] = total
    for f in range(FEATURES):
        pooled_ref[:, f * EMB : (f + 1) * EMB] = rows_ref[
            pl.ds(f, OWN, stride=FEATURES), :
        ].astype(BF16)
    for tower, (layer_ref, head_ref) in enumerate(((layer0_ref, head0_ref), (layer1_ref, head1_ref))):
        pooled = pooled_ref[:, tower * IN_WIDTH : (tower + 1) * IN_WIDTH]
        pre = dot(pooled, layer_ref[...])
        hidden = (pre * (1.0 / (1.0 + jnp.exp(-pre)))).astype(BF16)
        output = dot(hidden, head_ref[...])
        scale = lax.rsqrt(jnp.sum(output * output, axis=-1, keepdims=True) + EPSILON)
        unit = output * scale
        pre_ref[:, tower * HID : (tower + 1) * HID] = pre
        hidden_ref[:, tower * HID : (tower + 1) * HID] = hidden
        unit_ref[:, tower * OUT : (tower + 1) * OUT] = unit
        scale_ref[:, tower * OUT : (tower + 1) * OUT] = jnp.broadcast_to(scale, (OWN, OUT))
        rounded = unit.astype(BF16)
        for d in range(N_DP):
            send_ref[d, tower * OWN : (tower + 1) * OWN, :] = rounded
    counts = column_of(counts_ref[...].astype(F32))
    spread = jnp.broadcast_to(counts, (OWN, 128)).astype(BF16)
    for d in range(N_DP):
        send_ref[d, 2 * OWN : 3 * OWN, :] = spread


def towers(parts, counts, layer0, head0, layer1, head1):
    return pl.pallas_call(
        tower_kernel,
        in_specs=[whole()] * 6,
        out_specs=[whole()] * 6,
        out_shape=[
            jax.ShapeDtypeStruct((OWN, FEATURES * EMB), BF16),
            jax.ShapeDtypeStruct((OWN, 2 * HID), F32),
            jax.ShapeDtypeStruct((OWN, 2 * HID), BF16),
            jax.ShapeDtypeStruct((OWN, 2 * OUT), F32),
            jax.ShapeDtypeStruct((OWN, 2 * OUT), F32),
            jax.ShapeDtypeStruct((N_DP, 3 * OWN, 128), BF16),
        ],
        scratch_shapes=[pltpu.VMEM((BLOCK, EMB), F32)],
        compiler_params=PARAMS,
        name="towers",
    )(parts, counts, layer0, head0, layer1, head1)


def softmax_kernel(
    place_ref, group_ref, counts_ref, pooled_ref, pre_ref, hidden_ref, unit_ref, scale_ref,
    head0_ref, head1_ref, losses_ref, send_ref,
):
    size = N_DP * OWN
    group = group_ref[...]
    users = group[:, :OWN].reshape(size, OUT)
    items = group[:, OWN : 2 * OWN].reshape(size, OUT)
    log_freq = jnp.log(group[:, 2 * OWN :].reshape(size, 128).astype(F32))
    log_row = jnp.transpose(log_freq)[:1]
    own_log = jnp.log(column_of(counts_ref[...].astype(F32)))
    own_user = unit_ref[:, :OUT].astype(BF16)
    own_item = unit_ref[:, OUT:].astype(BF16)
    first = place_ref[0] * OWN
    mine = lax.broadcasted_iota(jnp.int32, (OWN, size), 1) == (
        lax.broadcasted_iota(jnp.int32, (OWN, size), 0) + first
    )
    down = INVERSE_TEMP * dot(items, users, NT) - jnp.concatenate([log_freq, log_freq], axis=1)
    lse_row = jnp.log(jnp.sum(jnp.exp(down), axis=0, keepdims=True))
    scores = INVERSE_TEMP * dot(own_user, items, NT) - log_row
    lse = jnp.log(jnp.sum(jnp.exp(scores), axis=1, keepdims=True))
    positive = jnp.sum(jnp.where(mine, scores, 0.0), axis=1, keepdims=True)
    losses_ref[...] = row_of(lse - positive)
    hot = mine.astype(F32)
    d_user = INVERSE_TEMP * dot((jnp.exp(scores - lse) - hot).astype(BF16), items)
    own_down = INVERSE_TEMP * dot(own_item, users, NT) - own_log
    d_item = INVERSE_TEMP * dot((jnp.exp(own_down - lse_row) - hot).astype(BF16), users)
    common = []
    outputs = []
    for tower, (d_unit, head_ref) in enumerate(((d_user, head0_ref), (d_item, head1_ref))):
        unit = unit_ref[:, tower * OUT : (tower + 1) * OUT]
        scale = scale_ref[:, tower * OUT : (tower + 1) * OUT]
        along = jnp.sum(unit * d_unit, axis=-1, keepdims=True)
        d_output = ((d_unit - unit * along) * scale).astype(BF16)
        pre = pre_ref[:, tower * HID : (tower + 1) * HID]
        gate = 1.0 / (1.0 + jnp.exp(-pre))
        slope = gate * (1.0 + pre * (1.0 - gate))
        common.append((dot(d_output, head_ref[...], NT) * slope).astype(BF16))
        outputs.append(d_output)
    common = jnp.concatenate(common + outputs, axis=1)
    pooled = pooled_ref[...]
    hidden = hidden_ref[...]
    blank = jnp.zeros((OWN, 64), BF16)
    for chip in range(N_CHIP):
        send_ref[chip, :, :COLUMNS_AT] = common
        send_ref[chip, :, COLUMNS_AT:] = jnp.concatenate(
            [
                pooled[:, chip * 64 : chip * 64 + 64],
                pooled[:, IN_WIDTH + chip * 64 : IN_WIDTH + chip * 64 + 64],
                hidden[:, chip * 32 : chip * 32 + 32],
                hidden[:, HID + chip * 32 : HID + chip * 32 + 32],
                blank,
            ],
            axis=1,
        )


def softmax_back(place, group, counts, pooled, pre, hidden, unit, scale, head0, head1):
    return pl.pallas_call(
        softmax_kernel,
        in_specs=[pl.BlockSpec(memory_space=pltpu.SMEM)] + [whole()] * 9,
        out_specs=[whole()] * 2,
        out_shape=[
            jax.ShapeDtypeStruct((1, OWN), F32),
            jax.ShapeDtypeStruct((N_CHIP, OWN, GRAD_WIDTH), BF16),
        ],
        compiler_params=PARAMS,
        name="softmax_back",
    )(place, group, counts, pooled, pre, hidden, unit, scale, head0, head1)


def back_kernel(first, *refs):
    core_ref, grads_ref, weights_ref, layer0_ref, layer1_ref = refs[:5]
    if first:
        total_ref, layers_ref, heads_ref, pooled_ref, here_ref, sems = refs[5:]
    else:
        before_ref, layers_before_ref, heads_before_ref = refs[5:8]
        send_ref, pooled_ref, here_ref, layers_ref, heads_ref, sems = refs[8:]
    samples = N_CHIP * OWN
    rows = samples * FEATURES // BACK_PARTS

    def copy(part):
        at = pl.ds(part * rows, rows)
        return pltpu.make_async_copy(weights_ref.at[at, :], here_ref.at[at, :], sems.at[part])

    for part in range(BACK_PARTS):
        copy(part).start()
    grads = grads_ref[...].reshape(samples, GRAD_WIDTH)
    inputs = grads[:, COLUMNS_AT : COLUMNS_AT + 128]
    hidden = grads[:, COLUMNS_AT + 128 :]
    d_hidden = (grads[:, :HID], grads[:, HID : 2 * HID])
    for f in range(FEATURES):
        tower = f // TOWER_FEATURES
        layer_ref = (layer0_ref, layer1_ref)[tower]
        at = (f % TOWER_FEATURES) * EMB
        pooled_ref[pl.ds(f, samples, stride=FEATURES), :] = dot(
            d_hidden[tower], layer_ref[at : at + EMB, :], NT
        )
    for tower in range(2):
        d_output = grads[:, 2 * HID + tower * OUT : 2 * HID + (tower + 1) * OUT]
        layer_rows = dot(inputs, d_hidden[tower], TN)[tower * 64 : tower * 64 + 64]
        head_rows = dot(hidden, d_output, TN)[tower * 32 : tower * 32 + 32]
        if not first:
            layer_rows = layer_rows + layers_before_ref[tower]
            head_rows = head_rows + heads_before_ref[tower]
        layers_ref[tower] = layer_rows
        heads_ref[tower] = head_rows
    total = None if first else before_ref[...]
    for part in range(BACK_PARTS):
        copy(part).wait()
        at = pl.ds(part * rows, rows)
        term = dot(pooled_ref[at, :].astype(BF16), here_ref[at, :], TN)
        total = term if total is None else total + term
    if first:
        total_ref[...] = total
        return
    table_rows = jnp.transpose(total)
    core = core_ref[0]
    for d in range(N_DP):
        send_ref[d, :64, :] = table_rows[d * 64 : (d + 1) * 64].astype(BF16)
        tower, quarter, half = d // 8, d % 8 // 2, d % 2
        send_ref[d, 64:80, :] = layers_ref[
            tower,
            pl.ds(pl.multiple_of(core * 32 + half * 16, 16), 16),
            quarter * 128 : quarter * 128 + 128,
        ].astype(BF16)
        if d < 2:
            send_ref[d, 80:, :] = heads_ref[d, pl.ds(pl.multiple_of(core * 16, 16), 16), :].astype(BF16)
        else:
            send_ref[d, 80:, :] = jnp.zeros((16, 128), BF16)


def back(core, grads, weights, layer0, layer1, before=None):
    first = before is None
    total = jax.ShapeDtypeStruct((EMB, ROWS), F32)
    layers = jax.ShapeDtypeStruct((2, 64, HID), F32)
    heads = jax.ShapeDtypeStruct((2, 32, OUT), F32)
    scratch = [pltpu.VMEM((N_CHIP * BLOCK, EMB), F32), pltpu.VMEM((N_CHIP * BLOCK, ROWS), BF16)]
    if first:
        out_shape = [total, layers, heads]
    else:
        out_shape = [jax.ShapeDtypeStruct((N_DP, CHUNK, 128), BF16)]
        scratch += [pltpu.VMEM(layers.shape, F32), pltpu.VMEM(heads.shape, F32)]
    before = before or ()
    return pl.pallas_call(
        lambda *refs: back_kernel(first, *refs),
        in_specs=[
            pl.BlockSpec(memory_space=pltpu.SMEM),
            whole(),
            pl.BlockSpec(memory_space=pl.ANY),
            whole(),
            whole(),
        ]
        + [whole()] * len(before),
        out_specs=[whole()] * len(out_shape),
        out_shape=out_shape,
        scratch_shapes=scratch + [pltpu.SemaphoreType.DMA((BACK_PARTS,))],
        compiler_params=PARAMS,
        cost_estimate=pl.CostEstimate(
            flops=2 * N_CHIP * BLOCK * ROWS * EMB, bytes_accessed=10 * 2**20, transcendentals=0
        ),
        name="back",
    )(core, grads, weights, layer0, layer1, *before)


def sum_kernel(parts_ref, send_ref):
    total = parts_ref[0].astype(F32)
    for d in range(1, N_DP):
        total = total + parts_ref[d].astype(F32)
    total = total.astype(BF16)
    for d in range(N_DP):
        send_ref[d] = total


def sum_parts(parts):
    return pl.pallas_call(
        sum_kernel,
        in_specs=[whole()],
        out_specs=whole(),
        out_shape=jax.ShapeDtypeStruct(parts.shape, BF16),
        compiler_params=PARAMS,
        name="sum_parts",
    )(parts)


def spread_kernel(sums_ref, table_ref, layer0_ref, head0_ref, layer1_ref, head1_ref):
    for d in range(N_DP):
        table_ref[d * 64 : (d + 1) * 64, :] = sums_ref[d, :64, :].astype(F32)
        tower, quarter, half = d // 8, d % 8 // 2, d % 2
        (layer0_ref, layer1_ref)[tower][
            half * 16 : half * 16 + 16, quarter * 128 : quarter * 128 + 128
        ] = sums_ref[d, 64:80, :].astype(F32)
    head0_ref[...] = sums_ref[0, 80:, :].astype(F32)
    head1_ref[...] = sums_ref[1, 80:, :].astype(F32)


def spread(sums):
    return pl.pallas_call(
        spread_kernel,
        in_specs=[whole()],
        out_specs=[whole()] * 5,
        out_shape=[
            jax.ShapeDtypeStruct((ROWS, EMB), F32),
            jax.ShapeDtypeStruct((32, HID), F32),
            jax.ShapeDtypeStruct((16, OUT), F32),
            jax.ShapeDtypeStruct((32, HID), F32),
            jax.ShapeDtypeStruct((16, OUT), F32),
        ],
        compiler_params=PARAMS,
        name="spread",
    )(sums)


def exchange(values, axes):
    return lax.all_to_all(values, axes, 0, 0, tiled=True)


def to_other_core(values):
    return lax.ppermute(values, "core", [(0, 1), (1, 0)])


def shards(ids, mults, table, user_layer, user_head, item_layer, item_head, counts):
    core = lax.axis_index("core").reshape(1)
    place = lax.axis_index(DP).reshape(1)
    ids = ids[0].reshape(N_CHIP, 2, OWN, 128)
    mults = mults[0].reshape(N_CHIP, 2, OWN, 128)

    def of_core(values, which):
        return lax.dynamic_index_in_dim(values, which, 1, False).reshape(N_CHIP * OWN, 128)

    other_weights, other_partial = pool(of_core(ids, 1 - core[0]), of_core(mults, 1 - core[0]), table)
    arrived = to_other_core(other_partial)
    own_weights, own_partial = pool(of_core(ids, core[0]), of_core(mults, core[0]), table)
    chip_partial = (own_partial.astype(F32) + arrived.astype(F32)).astype(BF16)
    parts = exchange(chip_partial.reshape(N_CHIP, BLOCK, EMB), CHIPS)
    pooled, pre, hidden, unit, scale, units = towers(
        parts, counts, user_layer, user_head, item_layer, item_head
    )
    group = exchange(units, DP)
    losses, grads = softmax_back(
        place, group, counts, pooled, pre, hidden, unit, scale, user_head, item_head
    )
    own_grads = exchange(grads, CHIPS)
    other_grads = to_other_core(own_grads)
    before = back(core, own_grads, own_weights, user_layer, item_layer)
    (terms,) = back(core, other_grads, other_weights, user_layer, item_layer, tuple(before))
    sums = exchange(sum_parts(exchange(terms, DP)), DP)
    table_change, layer0, head0, layer1, head1 = spread(sums)
    return (losses, table_change, layer0, head0, layer1, head1)


def solution(mesh):
    fine = Mesh(mesh.devices.reshape(tuple(AXES.values())), tuple(AXES))
    in_specs = (
        P(TABLE, DP, None),
        P(TABLE, DP, None),
        P(TABLE, None),
        P(),
        P(),
        P(),
        P(),
        P(DP, TABLE),
    )
    out_specs = (P(DP, TABLE),) + (P(TABLE, None),) * 5
    return jax.shard_map(shards, mesh=fine, in_specs=in_specs, out_specs=out_specs, check_vma=False)
```

```python
import jax
import jax.numpy as jnp
from jax import lax
from jax.experimental import pallas as pl
from jax.experimental.pallas import tpu as pltpu
from jax.sharding import Mesh
from jax.sharding import PartitionSpec as P

LOOKUPS = 8
INVERSE_TEMP = 20.0
EPSILON = 1e-06

AXES = {"x_lo": 2, "z": 8, "core": 2, "x_hi": 2, "y": 8}
TABLE = ("x_lo", "z", "core")
CHIPS = ("x_lo", "z")
DP = ("x_hi", "y")
N_CHIP = 16
N_DP = 16
OWN = 16
FEATURES = 16
TOWER_FEATURES = 8
ROWS = 1024
EMB = 128
HID = 512
OUT = 128
BLOCK = OWN * FEATURES
IN_WIDTH = TOWER_FEATURES * EMB
GRAD_WIDTH = 12 * 128
COLUMNS_AT = 2 * HID + 2 * OUT
POOL_SAMPLES = 64
BACK_PARTS = 4
CHUNK = 88

BF16 = jnp.bfloat16
F32 = jnp.float32

NT = (((1,), (1,)), ((), ()))
TN = (((0,), (0,)), ((), ()))


def dot(left, right, dims=(((1,), (0,)), ((), ()))):
    return lax.dot_general(left, right, dims, preferred_element_type=F32)


def room(mib):
    return pltpu.CompilerParams(vmem_limit_bytes=mib * 2**20)


def whole():
    return pl.BlockSpec(memory_space=pltpu.VMEM)


def lookup_weights(ids, mults, weights_ref, first):
    lane = lax.broadcasted_iota(jnp.int32, ids.shape, 1)
    high = lax.shift_right_logical(ids, 7) * FEATURES + lax.shift_right_logical(lane, 3)
    high = high.astype(F32)
    low = jnp.transpose((ids & 127).astype(F32))
    mults = mults.astype(F32)
    down = lax.broadcasted_iota(jnp.int32, (128, 128), 0).astype(F32).astype(BF16)
    across = lax.broadcasted_iota(jnp.int32, (128, 128), 1).astype(F32).astype(BF16)
    zero = jnp.zeros((128, 128), BF16)
    one = jnp.ones((128, 128), BF16)

    def spread_row(values, n):
        row = jnp.broadcast_to(values[n : n + 1], (16, 128)).astype(BF16)
        return jnp.concatenate([row] * 8, axis=0)

    for n in range(ids.shape[0]):
        left = jnp.where(spread_row(high, n) == down, spread_row(mults, n), zero)
        spread_low = jnp.broadcast_to(low[:, n : n + 1], (128, 128)).astype(BF16)
        right = jnp.where(spread_low == across, one, zero)
        hits = dot(left, right).astype(BF16)
        at = first + n * FEATURES
        for h in range(8):
            weights_ref[at : at + FEATURES, h * 128 : (h + 1) * 128] = hits[
                h * FEATURES : (h + 1) * FEATURES
            ]


def pool_kernel(other, place_ref, lookups_ref, table_ref, weights_ref, partial_ref):
    core = place_ref[0] ^ other
    parts = N_CHIP * OWN // POOL_SAMPLES
    rows = POOL_SAMPLES * FEATURES

    def sum_part(part):
        at = pl.ds(part * rows, rows)
        partial_ref[at, :] = dot(weights_ref[at, :], table_ref[...]).astype(BF16)

    for part in range(parts):
        chips = range(part * POOL_SAMPLES // OWN, (part + 1) * POOL_SAMPLES // OWN)
        starts = [pl.multiple_of((2 * chip + core) * OWN, OWN) for chip in chips]
        lookups = jnp.concatenate([lookups_ref[pl.ds(start, OWN), :] for start in starts], axis=0)
        lookup_weights(lookups & 1023, lax.shift_right_logical(lookups, 10), weights_ref, part * rows)
        if part > 0:
            sum_part(part - 1)
    sum_part(parts - 1)


def pool(other, place, lookups, table):
    return pl.pallas_call(
        lambda *refs: pool_kernel(other, *refs),
        in_specs=[pl.BlockSpec(memory_space=pltpu.SMEM)] + [whole()] * 2,
        out_specs=[whole()] * 2,
        out_shape=[
            jax.ShapeDtypeStruct((N_CHIP * BLOCK, ROWS), BF16),
            jax.ShapeDtypeStruct((N_CHIP * BLOCK, EMB), BF16),
        ],
        compiler_params=room(8),
        cost_estimate=pl.CostEstimate(
            flops=2 * N_CHIP * BLOCK * ROWS * EMB * 2, bytes_accessed=10 * 2**20, transcendentals=0
        ),
        name="pool",
    )(place, lookups, table)


def column_of(row):
    eye = lax.broadcasted_iota(jnp.int32, (OWN, OWN), 0) == lax.broadcasted_iota(
        jnp.int32, (OWN, OWN), 1
    )
    return jnp.sum(jnp.where(eye, row, 0.0), axis=1, keepdims=True)


def row_of(column):
    eye = lax.broadcasted_iota(jnp.int32, (OWN, OWN), 0) == lax.broadcasted_iota(
        jnp.int32, (OWN, OWN), 1
    )
    return jnp.sum(jnp.where(eye, column, 0.0), axis=0, keepdims=True)


def tower_kernel(
    parts_ref, counts_ref, layer0_ref, head0_ref, layer1_ref, head1_ref,
    pooled_ref, pre_ref, hidden_ref, unit_ref, scale_ref, send_ref, rows_ref,
):
    total = parts_ref[0].astype(F32)
    for s in range(1, N_CHIP):
        total = total + parts_ref[s].astype(F32)
    rows_ref[...] = total
    for f in range(FEATURES):
        pooled_ref[:, f * EMB : (f + 1) * EMB] = rows_ref[
            pl.ds(f, OWN, stride=FEATURES), :
        ].astype(BF16)
    for tower, (layer_ref, head_ref) in enumerate(((layer0_ref, head0_ref), (layer1_ref, head1_ref))):
        pooled = pooled_ref[:, tower * IN_WIDTH : (tower + 1) * IN_WIDTH]
        pre = dot(pooled, layer_ref[...])
        hidden = (pre * (1.0 / (1.0 + jnp.exp(-pre)))).astype(BF16)
        output = dot(hidden, head_ref[...])
        scale = lax.rsqrt(jnp.sum(output * output, axis=-1, keepdims=True) + EPSILON)
        unit = output * scale
        pre_ref[:, tower * HID : (tower + 1) * HID] = pre
        hidden_ref[:, tower * HID : (tower + 1) * HID] = hidden
        unit_ref[:, tower * OUT : (tower + 1) * OUT] = unit
        scale_ref[:, tower * OUT : (tower + 1) * OUT] = jnp.broadcast_to(scale, (OWN, OUT))
        rounded = unit.astype(BF16)
        for d in range(N_DP):
            send_ref[d, tower * OWN : (tower + 1) * OWN, :] = rounded
    counts = column_of(counts_ref[...].astype(F32))
    spread = jnp.broadcast_to(counts, (OWN, 128)).astype(BF16)
    for d in range(N_DP):
        send_ref[d, 2 * OWN : 3 * OWN, :] = spread


def towers(parts, counts, layer0, head0, layer1, head1):
    return pl.pallas_call(
        tower_kernel,
        in_specs=[whole()] * 6,
        out_specs=[whole()] * 6,
        out_shape=[
            jax.ShapeDtypeStruct((OWN, FEATURES * EMB), BF16),
            jax.ShapeDtypeStruct((OWN, 2 * HID), F32),
            jax.ShapeDtypeStruct((OWN, 2 * HID), BF16),
            jax.ShapeDtypeStruct((OWN, 2 * OUT), F32),
            jax.ShapeDtypeStruct((OWN, 2 * OUT), F32),
            jax.ShapeDtypeStruct((N_DP, 3 * OWN, 128), BF16),
        ],
        scratch_shapes=[pltpu.VMEM((BLOCK, EMB), F32)],
        compiler_params=room(8),
        name="towers",
    )(parts, counts, layer0, head0, layer1, head1)


def softmax_kernel(
    place_ref, group_ref, counts_ref, pooled_ref, pre_ref, hidden_ref, unit_ref, scale_ref,
    head0_ref, head1_ref, losses_ref, send_ref,
):
    size = N_DP * OWN
    group = group_ref[...]
    users = group[:, :OWN].reshape(size, OUT)
    items = group[:, OWN : 2 * OWN].reshape(size, OUT)
    log_freq = jnp.log(group[:, 2 * OWN :].reshape(size, 128).astype(F32))
    log_row = jnp.transpose(log_freq)[:1]
    own_log = jnp.log(column_of(counts_ref[...].astype(F32)))
    own_user = unit_ref[:, :OUT].astype(BF16)
    own_item = unit_ref[:, OUT:].astype(BF16)
    first = place_ref[1] * OWN
    mine = lax.broadcasted_iota(jnp.int32, (OWN, size), 1) == (
        lax.broadcasted_iota(jnp.int32, (OWN, size), 0) + first
    )
    down = INVERSE_TEMP * dot(items, users, NT) - jnp.concatenate([log_freq, log_freq], axis=1)
    lse_row = jnp.log(jnp.sum(jnp.exp(down), axis=0, keepdims=True))
    scores = INVERSE_TEMP * dot(own_user, items, NT) - log_row
    lse = jnp.log(jnp.sum(jnp.exp(scores), axis=1, keepdims=True))
    positive = jnp.sum(jnp.where(mine, scores, 0.0), axis=1, keepdims=True)
    losses_ref[...] = row_of(lse - positive)
    hot = mine.astype(F32)
    d_user = INVERSE_TEMP * dot((jnp.exp(scores - lse) - hot).astype(BF16), items)
    own_down = INVERSE_TEMP * dot(own_item, users, NT) - own_log
    d_item = INVERSE_TEMP * dot((jnp.exp(own_down - lse_row) - hot).astype(BF16), users)
    common = []
    outputs = []
    for tower, (d_unit, head_ref) in enumerate(((d_user, head0_ref), (d_item, head1_ref))):
        unit = unit_ref[:, tower * OUT : (tower + 1) * OUT]
        scale = scale_ref[:, tower * OUT : (tower + 1) * OUT]
        along = jnp.sum(unit * d_unit, axis=-1, keepdims=True)
        d_output = ((d_unit - unit * along) * scale).astype(BF16)
        pre = pre_ref[:, tower * HID : (tower + 1) * HID]
        gate = 1.0 / (1.0 + jnp.exp(-pre))
        slope = gate * (1.0 + pre * (1.0 - gate))
        common.append((dot(d_output, head_ref[...], NT) * slope).astype(BF16))
        outputs.append(d_output)
    common = jnp.concatenate(common + outputs, axis=1)
    pooled = pooled_ref[...]
    hidden = hidden_ref[...]
    blank = jnp.zeros((OWN, 64), BF16)
    for chip in range(N_CHIP):
        send_ref[chip, :, :COLUMNS_AT] = common
        send_ref[chip, :, COLUMNS_AT:] = jnp.concatenate(
            [
                pooled[:, chip * 64 : chip * 64 + 64],
                pooled[:, IN_WIDTH + chip * 64 : IN_WIDTH + chip * 64 + 64],
                hidden[:, chip * 32 : chip * 32 + 32],
                hidden[:, HID + chip * 32 : HID + chip * 32 + 32],
                blank,
            ],
            axis=1,
        )


def softmax_back(place, group, counts, pooled, pre, hidden, unit, scale, head0, head1):
    return pl.pallas_call(
        softmax_kernel,
        in_specs=[pl.BlockSpec(memory_space=pltpu.SMEM)] + [whole()] * 9,
        out_specs=[whole()] * 2,
        out_shape=[
            jax.ShapeDtypeStruct((1, OWN), F32),
            jax.ShapeDtypeStruct((N_CHIP, OWN, GRAD_WIDTH), BF16),
        ],
        compiler_params=room(6),
        name="softmax_back",
    )(place, group, counts, pooled, pre, hidden, unit, scale, head0, head1)


def back_kernel(first, *refs):
    place_ref, grads_ref, weights_ref, layer0_ref, layer1_ref = refs[:5]
    if first:
        total_ref, layers_ref, heads_ref, pooled_ref = refs[5:]
    else:
        before_ref, layers_before_ref, heads_before_ref = refs[5:8]
        send_ref, pooled_ref, layers_ref, heads_ref = refs[8:]
    samples = N_CHIP * OWN
    rows = samples * FEATURES // BACK_PARTS
    grads = grads_ref[...].reshape(samples, GRAD_WIDTH)
    inputs = grads[:, COLUMNS_AT : COLUMNS_AT + 128]
    hidden = grads[:, COLUMNS_AT + 128 :]
    d_hidden = (grads[:, :HID], grads[:, HID : 2 * HID])
    for f in range(FEATURES):
        tower = f // TOWER_FEATURES
        layer_ref = (layer0_ref, layer1_ref)[tower]
        at = (f % TOWER_FEATURES) * EMB
        pooled_ref[pl.ds(f, samples, stride=FEATURES), :] = dot(
            d_hidden[tower], layer_ref[at : at + EMB, :], NT
        )
    for tower in range(2):
        d_output = grads[:, 2 * HID + tower * OUT : 2 * HID + (tower + 1) * OUT]
        layer_rows = dot(inputs, d_hidden[tower], TN)[tower * 64 : tower * 64 + 64]
        head_rows = dot(hidden, d_output, TN)[tower * 32 : tower * 32 + 32]
        if not first:
            layer_rows = layer_rows + layers_before_ref[tower]
            head_rows = head_rows + heads_before_ref[tower]
        layers_ref[tower] = layer_rows
        heads_ref[tower] = head_rows
    total = None if first else before_ref[...]
    for part in range(BACK_PARTS):
        at = pl.ds(part * rows, rows)
        term = dot(pooled_ref[at, :].astype(BF16), weights_ref[at, :], TN)
        total = term if total is None else total + term
    if first:
        total_ref[...] = total
        return
    table_rows = jnp.transpose(total)
    core = place_ref[0]
    for d in range(N_DP):
        send_ref[d, :64, :] = table_rows[d * 64 : (d + 1) * 64].astype(BF16)
        tower, quarter, half = d // 8, d % 8 // 2, d % 2
        send_ref[d, 64:80, :] = layers_ref[
            tower,
            pl.ds(pl.multiple_of(core * 32 + half * 16, 16), 16),
            quarter * 128 : quarter * 128 + 128,
        ].astype(BF16)
        if d < 4:
            at = pl.multiple_of(core * 16 + d % 2 * 8, 8)
            send_ref[d, 80:, :] = heads_ref[d // 2, pl.ds(at, 8), :].astype(BF16)
        else:
            send_ref[d, 80:, :] = jnp.zeros((8, 128), BF16)


def back(place, grads, weights, layer0, layer1, before=None):
    first = before is None
    total = jax.ShapeDtypeStruct((EMB, ROWS), F32)
    layers = jax.ShapeDtypeStruct((2, 64, HID), F32)
    heads = jax.ShapeDtypeStruct((2, 32, OUT), F32)
    scratch = [pltpu.VMEM((N_CHIP * BLOCK, EMB), F32)]
    if first:
        out_shape = [total, layers, heads]
    else:
        out_shape = [jax.ShapeDtypeStruct((N_DP, CHUNK, 128), BF16)]
        scratch += [pltpu.VMEM(layers.shape, F32), pltpu.VMEM(heads.shape, F32)]
    before = before or ()
    return pl.pallas_call(
        lambda *refs: back_kernel(first, *refs),
        in_specs=[
            pl.BlockSpec(memory_space=pltpu.SMEM),
        ]
        + [whole()] * (4 + len(before)),
        out_specs=[whole()] * len(out_shape),
        out_shape=out_shape,
        scratch_shapes=scratch,
        compiler_params=room(12),
        cost_estimate=pl.CostEstimate(
            flops=2 * N_CHIP * BLOCK * ROWS * EMB, bytes_accessed=10 * 2**20, transcendentals=0
        ),
        name="back",
    )(place, grads, weights, layer0, layer1, *before)


def sum_kernel(parts_ref, send_ref):
    total = parts_ref[0].astype(F32)
    for d in range(1, N_DP):
        total = total + parts_ref[d].astype(F32)
    total = total.astype(BF16)
    for d in range(N_DP):
        send_ref[d] = total


def sum_parts(parts):
    return pl.pallas_call(
        sum_kernel,
        in_specs=[whole()],
        out_specs=whole(),
        out_shape=jax.ShapeDtypeStruct(parts.shape, BF16),
        compiler_params=room(2),
        name="sum_parts",
    )(parts)


def spread_kernel(sums_ref, table_ref, layer0_ref, head0_ref, layer1_ref, head1_ref):
    for d in range(N_DP):
        table_ref[d * 64 : (d + 1) * 64, :] = sums_ref[d, :64, :].astype(F32)
        tower, quarter, half = d // 8, d % 8 // 2, d % 2
        (layer0_ref, layer1_ref)[tower][
            half * 16 : half * 16 + 16, quarter * 128 : quarter * 128 + 128
        ] = sums_ref[d, 64:80, :].astype(F32)
    for d in range(4):
        (head0_ref, head1_ref)[d // 2][d % 2 * 8 : d % 2 * 8 + 8, :] = sums_ref[d, 80:, :].astype(F32)


def spread(sums):
    return pl.pallas_call(
        spread_kernel,
        in_specs=[whole()],
        out_specs=[whole()] * 5,
        out_shape=[
            jax.ShapeDtypeStruct((ROWS, EMB), F32),
            jax.ShapeDtypeStruct((32, HID), F32),
            jax.ShapeDtypeStruct((16, OUT), F32),
            jax.ShapeDtypeStruct((32, HID), F32),
            jax.ShapeDtypeStruct((16, OUT), F32),
        ],
        compiler_params=room(4),
        name="spread",
    )(sums)


def exchange(values, axes):
    return lax.all_to_all(values, axes, 0, 0, tiled=True)


def to_other_core(values):
    return lax.ppermute(values, "core", [(0, 1), (1, 0)])


def shards(ids, mults, table, user_layer, user_head, item_layer, item_head, counts):
    place = jnp.stack([lax.axis_index("core"), lax.axis_index(DP)])
    lookups = ids[0] + 1024 * mults[0]
    other_weights, other_partial = pool(1, place, lookups, table)
    arrived = to_other_core(other_partial)
    own_weights, own_partial = pool(0, place, lookups, table)
    chip_partial = (own_partial.astype(F32) + arrived.astype(F32)).astype(BF16)
    parts = exchange(chip_partial.reshape(N_CHIP, BLOCK, EMB), CHIPS)
    pooled, pre, hidden, unit, scale, units = towers(
        parts, counts, user_layer, user_head, item_layer, item_head
    )
    group = exchange(units, DP)
    losses, grads = softmax_back(
        place, group, counts, pooled, pre, hidden, unit, scale, user_head, item_head
    )
    own_grads = exchange(grads, CHIPS)
    other_grads = to_other_core(own_grads)
    before = back(place, own_grads, own_weights, user_layer, item_layer)
    (terms,) = back(place, other_grads, other_weights, user_layer, item_layer, tuple(before))
    sums = exchange(sum_parts(exchange(terms, DP)), DP)
    table_change, layer0, head0, layer1, head1 = spread(sums)
    return (losses, table_change, layer0, head0, layer1, head1)


def solution(mesh):
    fine = Mesh(mesh.devices.reshape(tuple(AXES.values())), tuple(AXES))
    in_specs = (
        P(TABLE, DP, None),
        P(TABLE, DP, None),
        P(TABLE, None),
        P(),
        P(),
        P(),
        P(),
        P(DP, TABLE),
    )
    out_specs = (P(DP, TABLE),) + (P(TABLE, None),) * 5
    return jax.shard_map(shards, mesh=fine, in_specs=in_specs, out_specs=out_specs, check_vma=False)
```

```python
import jax
import jax.numpy as jnp
from jax import lax
from jax.experimental import pallas as pl
from jax.experimental.pallas import tpu as pltpu
from jax.sharding import Mesh
from jax.sharding import PartitionSpec as P

LOOKUPS = 8
INVERSE_TEMP = 20.0
EPSILON = 1e-06

AXES = {"x_lo": 2, "z": 8, "core": 2, "x_hi": 2, "y": 8}
TABLE = ("x_lo", "z", "core")
CHIPS = ("x_lo", "z")
DP = ("x_hi", "y")
N_CHIP = 16
N_Z = 8
N_DP = 16
OWN = 16
FEATURES = 16
TOWER_FEATURES = 8
ROWS = 1024
EMB = 128
HID = 512
OUT = 128
BLOCK = OWN * FEATURES
IN_WIDTH = TOWER_FEATURES * EMB
GRAD_WIDTH = 12 * 128
COLUMNS_AT = 2 * HID + 2 * OUT
POOL_SAMPLES = 32
BACK_PARTS = 2
CHUNK = 88

BF16 = jnp.bfloat16
F32 = jnp.float32

NT = (((1,), (1,)), ((), ()))
TN = (((0,), (0,)), ((), ()))


def dot(left, right, dims=(((1,), (0,)), ((), ()))):
    return lax.dot_general(left, right, dims, preferred_element_type=F32)


def room(mib):
    return pltpu.CompilerParams(vmem_limit_bytes=mib * 2**20)


def whole():
    return pl.BlockSpec(memory_space=pltpu.VMEM)


def lookup_weights(ids, mults, weights_ref, first):
    lane = lax.broadcasted_iota(jnp.int32, ids.shape, 1)
    high = lax.shift_right_logical(ids, 7) * FEATURES + lax.shift_right_logical(lane, 3)
    high = high.astype(F32)
    low = jnp.transpose((ids & 127).astype(F32))
    mults = mults.astype(F32)
    down = lax.broadcasted_iota(jnp.int32, (128, 128), 0).astype(F32).astype(BF16)
    across = lax.broadcasted_iota(jnp.int32, (128, 128), 1).astype(F32).astype(BF16)
    zero = jnp.zeros((128, 128), BF16)
    one = jnp.ones((128, 128), BF16)

    def spread_row(values, n):
        row = jnp.broadcast_to(values[n : n + 1], (16, 128)).astype(BF16)
        return jnp.concatenate([row] * 8, axis=0)

    for n in range(ids.shape[0]):
        left = jnp.where(spread_row(high, n) == down, spread_row(mults, n), zero)
        spread_low = jnp.broadcast_to(low[:, n : n + 1], (128, 128)).astype(BF16)
        right = jnp.where(spread_low == across, one, zero)
        hits = dot(left, right).astype(BF16)
        at = first + n * FEATURES
        for h in range(8):
            weights_ref[at : at + FEATURES, h * 128 : (h + 1) * 128] = hits[
                h * FEATURES : (h + 1) * FEATURES
            ]


def pool_kernel(other_x, other_core, place_ref, lookups_ref, table_ref, weights_ref, partial_ref):
    core = place_ref[0] ^ other_core
    x_lo = place_ref[2] ^ other_x
    parts = N_Z * OWN // POOL_SAMPLES
    rows = POOL_SAMPLES * FEATURES

    def sum_part(part):
        at = pl.ds(part * rows, rows)
        partial_ref[at, :] = dot(weights_ref[at, :], table_ref[...]).astype(BF16)

    for part in range(parts):
        chips = range(part * POOL_SAMPLES // OWN, (part + 1) * POOL_SAMPLES // OWN)
        starts = [pl.multiple_of((2 * (x_lo * N_Z + z) + core) * OWN, OWN) for z in chips]
        lookups = jnp.concatenate([lookups_ref[pl.ds(start, OWN), :] for start in starts], axis=0)
        lookup_weights(lookups & 1023, lax.shift_right_logical(lookups, 10), weights_ref, part * rows)
        if part > 0:
            sum_part(part - 1)
    sum_part(parts - 1)


def pool(other_x, other_core, place, lookups, table):
    return pl.pallas_call(
        lambda *refs: pool_kernel(other_x, other_core, *refs),
        in_specs=[pl.BlockSpec(memory_space=pltpu.SMEM)] + [whole()] * 2,
        out_specs=[whole()] * 2,
        out_shape=[
            jax.ShapeDtypeStruct((N_Z * BLOCK, ROWS), BF16),
            jax.ShapeDtypeStruct((N_Z * BLOCK, EMB), BF16),
        ],
        compiler_params=room(8),
        cost_estimate=pl.CostEstimate(
            flops=2 * N_Z * BLOCK * ROWS * EMB * 2, bytes_accessed=5 * 2**20, transcendentals=0
        ),
        name="pool",
    )(place, lookups, table)


def column_of(row):
    eye = lax.broadcasted_iota(jnp.int32, (OWN, OWN), 0) == lax.broadcasted_iota(
        jnp.int32, (OWN, OWN), 1
    )
    return jnp.sum(jnp.where(eye, row, 0.0), axis=1, keepdims=True)


def row_of(column):
    eye = lax.broadcasted_iota(jnp.int32, (OWN, OWN), 0) == lax.broadcasted_iota(
        jnp.int32, (OWN, OWN), 1
    )
    return jnp.sum(jnp.where(eye, column, 0.0), axis=0, keepdims=True)


def tower_kernel(
    parts_ref, counts_ref, layer0_ref, head0_ref, layer1_ref, head1_ref,
    pooled_ref, pre_ref, hidden_ref, unit_ref, scale_ref, send_ref, rows_ref,
):
    total = parts_ref[0].astype(F32)
    for s in range(1, N_Z):
        total = total + parts_ref[s].astype(F32)
    rows_ref[...] = total
    for f in range(FEATURES):
        pooled_ref[:, f * EMB : (f + 1) * EMB] = rows_ref[
            pl.ds(f, OWN, stride=FEATURES), :
        ].astype(BF16)
    for tower, (layer_ref, head_ref) in enumerate(((layer0_ref, head0_ref), (layer1_ref, head1_ref))):
        pooled = pooled_ref[:, tower * IN_WIDTH : (tower + 1) * IN_WIDTH]
        pre = dot(pooled, layer_ref[...])
        hidden = (pre * (1.0 / (1.0 + jnp.exp(-pre)))).astype(BF16)
        output = dot(hidden, head_ref[...])
        scale = lax.rsqrt(jnp.sum(output * output, axis=-1, keepdims=True) + EPSILON)
        unit = output * scale
        pre_ref[:, tower * HID : (tower + 1) * HID] = pre
        hidden_ref[:, tower * HID : (tower + 1) * HID] = hidden
        unit_ref[:, tower * OUT : (tower + 1) * OUT] = unit
        scale_ref[:, tower * OUT : (tower + 1) * OUT] = jnp.broadcast_to(scale, (OWN, OUT))
        rounded = unit.astype(BF16)
        for d in range(N_DP):
            send_ref[d, tower * OWN : (tower + 1) * OWN, :] = rounded
    counts = column_of(counts_ref[...].astype(F32))
    spread = jnp.broadcast_to(counts, (OWN, 128)).astype(BF16)
    for d in range(N_DP):
        send_ref[d, 2 * OWN : 3 * OWN, :] = spread


def towers(parts, counts, layer0, head0, layer1, head1):
    return pl.pallas_call(
        tower_kernel,
        in_specs=[whole()] * 6,
        out_specs=[whole()] * 6,
        out_shape=[
            jax.ShapeDtypeStruct((OWN, FEATURES * EMB), BF16),
            jax.ShapeDtypeStruct((OWN, 2 * HID), F32),
            jax.ShapeDtypeStruct((OWN, 2 * HID), BF16),
            jax.ShapeDtypeStruct((OWN, 2 * OUT), F32),
            jax.ShapeDtypeStruct((OWN, 2 * OUT), F32),
            jax.ShapeDtypeStruct((N_DP, 3 * OWN, 128), BF16),
        ],
        scratch_shapes=[pltpu.VMEM((BLOCK, EMB), F32)],
        compiler_params=room(8),
        name="towers",
    )(parts, counts, layer0, head0, layer1, head1)


def softmax_kernel(
    place_ref, group_ref, counts_ref, pooled_ref, pre_ref, hidden_ref, unit_ref, scale_ref,
    head0_ref, head1_ref, losses_ref, send_ref,
):
    size = N_DP * OWN
    group = group_ref[...]
    users = group[:, :OWN].reshape(size, OUT)
    items = group[:, OWN : 2 * OWN].reshape(size, OUT)
    log_freq = jnp.log(group[:, 2 * OWN :].reshape(size, 128).astype(F32))
    log_row = jnp.transpose(log_freq)[:1]
    own_log = jnp.log(column_of(counts_ref[...].astype(F32)))
    own_user = unit_ref[:, :OUT].astype(BF16)
    own_item = unit_ref[:, OUT:].astype(BF16)
    first = place_ref[1] * OWN
    mine = lax.broadcasted_iota(jnp.int32, (OWN, size), 1) == (
        lax.broadcasted_iota(jnp.int32, (OWN, size), 0) + first
    )
    down = INVERSE_TEMP * dot(items, users, NT) - jnp.concatenate([log_freq, log_freq], axis=1)
    lse_row = jnp.log(jnp.sum(jnp.exp(down), axis=0, keepdims=True))
    scores = INVERSE_TEMP * dot(own_user, items, NT) - log_row
    lse = jnp.log(jnp.sum(jnp.exp(scores), axis=1, keepdims=True))
    positive = jnp.sum(jnp.where(mine, scores, 0.0), axis=1, keepdims=True)
    losses_ref[...] = row_of(lse - positive)
    hot = mine.astype(F32)
    d_user = INVERSE_TEMP * dot((jnp.exp(scores - lse) - hot).astype(BF16), items)
    own_down = INVERSE_TEMP * dot(own_item, users, NT) - own_log
    d_item = INVERSE_TEMP * dot((jnp.exp(own_down - lse_row) - hot).astype(BF16), users)
    common = []
    outputs = []
    for tower, (d_unit, head_ref) in enumerate(((d_user, head0_ref), (d_item, head1_ref))):
        unit = unit_ref[:, tower * OUT : (tower + 1) * OUT]
        scale = scale_ref[:, tower * OUT : (tower + 1) * OUT]
        along = jnp.sum(unit * d_unit, axis=-1, keepdims=True)
        d_output = ((d_unit - unit * along) * scale).astype(BF16)
        pre = pre_ref[:, tower * HID : (tower + 1) * HID]
        gate = 1.0 / (1.0 + jnp.exp(-pre))
        slope = gate * (1.0 + pre * (1.0 - gate))
        common.append((dot(d_output, head_ref[...], NT) * slope).astype(BF16))
        outputs.append(d_output)
    common = jnp.concatenate(common + outputs, axis=1)
    pooled = pooled_ref[...]
    hidden = hidden_ref[...]
    blank = jnp.zeros((OWN, 64), BF16)
    for chip in range(N_CHIP):
        send_ref[chip, :, :COLUMNS_AT] = common
        send_ref[chip, :, COLUMNS_AT:] = jnp.concatenate(
            [
                pooled[:, chip * 64 : chip * 64 + 64],
                pooled[:, IN_WIDTH + chip * 64 : IN_WIDTH + chip * 64 + 64],
                hidden[:, chip * 32 : chip * 32 + 32],
                hidden[:, HID + chip * 32 : HID + chip * 32 + 32],
                blank,
            ],
            axis=1,
        )


def softmax_back(place, group, counts, pooled, pre, hidden, unit, scale, head0, head1):
    return pl.pallas_call(
        softmax_kernel,
        in_specs=[pl.BlockSpec(memory_space=pltpu.SMEM)] + [whole()] * 9,
        out_specs=[whole()] * 2,
        out_shape=[
            jax.ShapeDtypeStruct((1, OWN), F32),
            jax.ShapeDtypeStruct((N_CHIP, OWN, GRAD_WIDTH), BF16),
        ],
        compiler_params=room(6),
        name="softmax_back",
    )(place, group, counts, pooled, pre, hidden, unit, scale, head0, head1)


def back_kernel(first, *refs):
    place_ref, grads_ref, here_ref, there_ref, layer0_ref, layer1_ref = refs[:6]
    if first:
        total_ref, layers_ref, heads_ref, pooled_ref = refs[6:]
    else:
        before_ref, layers_before_ref, heads_before_ref = refs[6:9]
        send_ref, pooled_ref, layers_ref, heads_ref = refs[9:]
    samples = N_CHIP * OWN
    half = samples * FEATURES // 2
    rows = half // BACK_PARTS
    grads = grads_ref[...].reshape(samples, GRAD_WIDTH)
    inputs = grads[:, COLUMNS_AT : COLUMNS_AT + 128]
    hidden = grads[:, COLUMNS_AT + 128 :]
    d_hidden = (grads[:, :HID], grads[:, HID : 2 * HID])
    for f in range(FEATURES):
        tower = f // TOWER_FEATURES
        layer_ref = (layer0_ref, layer1_ref)[tower]
        at = (f % TOWER_FEATURES) * EMB
        pooled_ref[pl.ds(f, samples, stride=FEATURES), :] = dot(
            d_hidden[tower], layer_ref[at : at + EMB, :], NT
        )
    for tower in range(2):
        d_output = grads[:, 2 * HID + tower * OUT : 2 * HID + (tower + 1) * OUT]
        layer_rows = dot(inputs, d_hidden[tower], TN)[tower * 64 : tower * 64 + 64]
        head_rows = dot(hidden, d_output, TN)[tower * 32 : tower * 32 + 32]
        if not first:
            layer_rows = layer_rows + layers_before_ref[tower]
            head_rows = head_rows + heads_before_ref[tower]
        layers_ref[tower] = layer_rows
        heads_ref[tower] = head_rows
    total = None if first else before_ref[...]
    for other_x, weights_ref in enumerate((here_ref, there_ref)):
        first_row = (place_ref[2] ^ other_x) * half
        for part in range(BACK_PARTS):
            at = pl.ds(pl.multiple_of(first_row + part * rows, rows), rows)
            weights = weights_ref[part * rows : (part + 1) * rows, :]
            term = dot(pooled_ref[at, :].astype(BF16), weights, TN)
            total = term if total is None else total + term
    if first:
        total_ref[...] = total
        return
    table_rows = jnp.transpose(total)
    core = place_ref[0]
    for d in range(N_DP):
        send_ref[d, :64, :] = table_rows[d * 64 : (d + 1) * 64].astype(BF16)
        tower, quarter, half = d // 8, d % 8 // 2, d % 2
        send_ref[d, 64:80, :] = layers_ref[
            tower,
            pl.ds(pl.multiple_of(core * 32 + half * 16, 16), 16),
            quarter * 128 : quarter * 128 + 128,
        ].astype(BF16)
        if d < 4:
            at = pl.multiple_of(core * 16 + d % 2 * 8, 8)
            send_ref[d, 80:, :] = heads_ref[d // 2, pl.ds(at, 8), :].astype(BF16)
        else:
            send_ref[d, 80:, :] = jnp.zeros((8, 128), BF16)


def back(place, grads, weights, layer0, layer1, before=None):
    first = before is None
    total = jax.ShapeDtypeStruct((EMB, ROWS), F32)
    layers = jax.ShapeDtypeStruct((2, 64, HID), F32)
    heads = jax.ShapeDtypeStruct((2, 32, OUT), F32)
    scratch = [pltpu.VMEM((N_CHIP * BLOCK, EMB), F32)]
    if first:
        out_shape = [total, layers, heads]
    else:
        out_shape = [jax.ShapeDtypeStruct((N_DP, CHUNK, 128), BF16)]
        scratch += [pltpu.VMEM(layers.shape, F32), pltpu.VMEM(heads.shape, F32)]
    before = before or ()
    return pl.pallas_call(
        lambda *refs: back_kernel(first, *refs),
        in_specs=[
            pl.BlockSpec(memory_space=pltpu.SMEM),
        ]
        + [whole()] * (5 + len(before)),
        out_specs=[whole()] * len(out_shape),
        out_shape=out_shape,
        scratch_shapes=scratch,
        compiler_params=room(12),
        cost_estimate=pl.CostEstimate(
            flops=2 * N_CHIP * BLOCK * ROWS * EMB, bytes_accessed=10 * 2**20, transcendentals=0
        ),
        name="back",
    )(place, grads, *weights, layer0, layer1, *before)


def sum_kernel(parts_ref, send_ref):
    total = parts_ref[0].astype(F32)
    for d in range(1, N_DP):
        total = total + parts_ref[d].astype(F32)
    total = total.astype(BF16)
    for d in range(N_DP):
        send_ref[d] = total


def sum_parts(parts):
    return pl.pallas_call(
        sum_kernel,
        in_specs=[whole()],
        out_specs=whole(),
        out_shape=jax.ShapeDtypeStruct(parts.shape, BF16),
        compiler_params=room(2),
        name="sum_parts",
    )(parts)


def spread_kernel(sums_ref, table_ref, layer0_ref, head0_ref, layer1_ref, head1_ref):
    for d in range(N_DP):
        table_ref[d * 64 : (d + 1) * 64, :] = sums_ref[d, :64, :].astype(F32)
        tower, quarter, half = d // 8, d % 8 // 2, d % 2
        (layer0_ref, layer1_ref)[tower][
            half * 16 : half * 16 + 16, quarter * 128 : quarter * 128 + 128
        ] = sums_ref[d, 64:80, :].astype(F32)
    for d in range(4):
        (head0_ref, head1_ref)[d // 2][d % 2 * 8 : d % 2 * 8 + 8, :] = sums_ref[d, 80:, :].astype(F32)


def spread(sums):
    return pl.pallas_call(
        spread_kernel,
        in_specs=[whole()],
        out_specs=[whole()] * 5,
        out_shape=[
            jax.ShapeDtypeStruct((ROWS, EMB), F32),
            jax.ShapeDtypeStruct((32, HID), F32),
            jax.ShapeDtypeStruct((16, OUT), F32),
            jax.ShapeDtypeStruct((32, HID), F32),
            jax.ShapeDtypeStruct((16, OUT), F32),
        ],
        compiler_params=room(4),
        name="spread",
    )(sums)


def exchange(values, axes):
    return lax.all_to_all(values, axes, 0, 0, tiled=True)


def to_other(values, axis):
    return lax.ppermute(values, axis, [(0, 1), (1, 0)])


def add(*terms):
    return sum(term.astype(F32) for term in terms).astype(BF16)


def shards(ids, mults, table, user_layer, user_head, item_layer, item_head, counts):
    place = jnp.stack([lax.axis_index("core"), lax.axis_index(DP), lax.axis_index("x_lo")])
    lookups = ids[0] + 1024 * mults[0]
    both_weights, both_partial = pool(1, 1, place, lookups, table)
    both_arrived = to_other(both_partial, "core")
    x_weights, x_partial = pool(1, 0, place, lookups, table)
    x_sum, lookups = lax.optimization_barrier((add(x_partial, both_arrived), lookups))
    x_arrived = to_other(x_sum, "x_lo")
    core_weights, core_partial = pool(0, 1, place, lookups, table)
    core_arrived = to_other(core_partial, "core")
    own_weights, own_partial = pool(0, 0, place, lookups, table)
    total_partial = add(own_partial, core_arrived, x_arrived)
    parts = exchange(total_partial.reshape(N_Z, BLOCK, EMB), "z")
    pooled, pre, hidden, unit, scale, units = towers(
        parts, counts, user_layer, user_head, item_layer, item_head
    )
    group = exchange(units, DP)
    losses, grads = softmax_back(
        place, group, counts, pooled, pre, hidden, unit, scale, user_head, item_head
    )
    own_grads = exchange(grads, CHIPS)
    other_grads = to_other(own_grads, "core")
    before = back(place, own_grads, (own_weights, x_weights), user_layer, item_layer)
    (terms,) = back(
        place, other_grads, (core_weights, both_weights), user_layer, item_layer, tuple(before)
    )
    sums = exchange(sum_parts(exchange(terms, DP)), DP)
    table_change, layer0, head0, layer1, head1 = spread(sums)
    return (losses, table_change, layer0, head0, layer1, head1)


def solution(mesh):
    fine = Mesh(mesh.devices.reshape(tuple(AXES.values())), tuple(AXES))
    in_specs = (
        P(TABLE, DP, None),
        P(TABLE, DP, None),
        P(TABLE, None),
        P(),
        P(),
        P(),
        P(),
        P(DP, TABLE),
    )
    out_specs = (P(DP, TABLE),) + (P(TABLE, None),) * 5
    return jax.shard_map(shards, mesh=fine, in_specs=in_specs, out_specs=out_specs, check_vma=False)
```

```python
import jax
import jax.numpy as jnp
from jax import lax
from jax.experimental import pallas as pl
from jax.experimental.pallas import tpu as pltpu
from jax.sharding import Mesh
from jax.sharding import PartitionSpec as P

LOOKUPS = 8
INVERSE_TEMP = 20.0
EPSILON = 1e-06

AXES = {"x_lo": 2, "z": 8, "core": 2, "x_hi": 2, "y": 8}
TABLE = ("x_lo", "z", "core")
CHIPS = ("x_lo", "z")
DP = ("x_hi", "y")
N_CHIP = 16
N_Z = 8
N_DP = 16
OWN = 16
FEATURES = 16
TOWER_FEATURES = 8
ROWS = 1024
EMB = 128
HID = 512
OUT = 128
BLOCK = OWN * FEATURES
IN_WIDTH = TOWER_FEATURES * EMB
GRAD_WIDTH = 12 * 128
COLUMNS_AT = 2 * HID + 2 * OUT
POOL_SAMPLES = 32
BACK_ROWS = 1024
CHUNK = 88

BF16 = jnp.bfloat16
F32 = jnp.float32

NT = (((1,), (1,)), ((), ()))
TN = (((0,), (0,)), ((), ()))


def dot(left, right, dims=(((1,), (0,)), ((), ()))):
    return lax.dot_general(left, right, dims, preferred_element_type=F32)


def room(mib):
    return pltpu.CompilerParams(vmem_limit_bytes=mib * 2**20)


def whole():
    return pl.BlockSpec(memory_space=pltpu.VMEM)


def lookup_weights(ids, mults, weights_ref, first):
    lane = lax.broadcasted_iota(jnp.int32, ids.shape, 1)
    high = lax.shift_right_logical(ids, 7) * FEATURES + lax.shift_right_logical(lane, 3)
    high = high.astype(F32)
    low = jnp.transpose((ids & 127).astype(F32))
    mults = mults.astype(F32)
    down = lax.broadcasted_iota(jnp.int32, (128, 128), 0).astype(F32).astype(BF16)
    across = lax.broadcasted_iota(jnp.int32, (128, 128), 1).astype(F32).astype(BF16)
    zero = jnp.zeros((128, 128), BF16)
    one = jnp.ones((128, 128), BF16)

    def spread_row(values, n):
        row = jnp.broadcast_to(values[n : n + 1], (16, 128)).astype(BF16)
        return jnp.concatenate([row] * 8, axis=0)

    for n in range(ids.shape[0]):
        left = jnp.where(spread_row(high, n) == down, spread_row(mults, n), zero)
        spread_low = jnp.broadcast_to(low[:, n : n + 1], (128, 128)).astype(BF16)
        right = jnp.where(spread_low == across, one, zero)
        hits = dot(left, right).astype(BF16)
        at = first + n * FEATURES
        for h in range(8):
            weights_ref[at : at + FEATURES, h * 128 : (h + 1) * 128] = hits[
                h * FEATURES : (h + 1) * FEATURES
            ]


def pool_kernel(groups, other_core, place_ref, lookups_ref, table_ref, weights_ref, partial_ref):
    core = place_ref[0] ^ other_core
    devices = [(other_x, z) for other_x, low, high in groups for z in range(low, high)]
    starts = [
        pl.multiple_of((2 * ((place_ref[2] ^ other_x) * N_Z + z) + core) * OWN, OWN)
        for other_x, z in devices
    ]
    together = POOL_SAMPLES // OWN
    parts = len(devices) // together
    rows = POOL_SAMPLES * FEATURES

    def sum_part(part):
        at = pl.ds(part * rows, rows)
        partial_ref[at, :] = dot(weights_ref[at, :], table_ref[...]).astype(BF16)

    for part in range(parts):
        here = starts[part * together : (part + 1) * together]
        lookups = jnp.concatenate([lookups_ref[pl.ds(start, OWN), :] for start in here], axis=0)
        lookup_weights(lookups & 1023, lax.shift_right_logical(lookups, 10), weights_ref, part * rows)
        if part > 0:
            sum_part(part - 1)
    sum_part(parts - 1)


def pool(groups, other_core, place, lookups, table):
    rows = sum(high - low for _, low, high in groups) * BLOCK
    return pl.pallas_call(
        lambda *refs: pool_kernel(groups, other_core, *refs),
        in_specs=[pl.BlockSpec(memory_space=pltpu.SMEM)] + [whole()] * 2,
        out_specs=[whole()] * 2,
        out_shape=[
            jax.ShapeDtypeStruct((rows, ROWS), BF16),
            jax.ShapeDtypeStruct((rows, EMB), BF16),
        ],
        compiler_params=room(8),
        cost_estimate=pl.CostEstimate(
            flops=2 * rows * ROWS * EMB * 2, bytes_accessed=rows * ROWS * 2, transcendentals=0
        ),
        name="pool",
    )(place, lookups, table)


def column_of(row):
    eye = lax.broadcasted_iota(jnp.int32, (OWN, OWN), 0) == lax.broadcasted_iota(
        jnp.int32, (OWN, OWN), 1
    )
    return jnp.sum(jnp.where(eye, row, 0.0), axis=1, keepdims=True)


def row_of(column):
    eye = lax.broadcasted_iota(jnp.int32, (OWN, OWN), 0) == lax.broadcasted_iota(
        jnp.int32, (OWN, OWN), 1
    )
    return jnp.sum(jnp.where(eye, column, 0.0), axis=0, keepdims=True)


def tower_kernel(
    parts_ref, counts_ref, layer0_ref, head0_ref, layer1_ref, head1_ref,
    pooled_ref, pre_ref, hidden_ref, unit_ref, scale_ref, send_ref, rows_ref,
):
    total = parts_ref[0].astype(F32)
    for s in range(1, N_Z):
        total = total + parts_ref[s].astype(F32)
    rows_ref[...] = total
    for f in range(FEATURES):
        pooled_ref[:, f * EMB : (f + 1) * EMB] = rows_ref[
            pl.ds(f, OWN, stride=FEATURES), :
        ].astype(BF16)
    for tower, (layer_ref, head_ref) in enumerate(((layer0_ref, head0_ref), (layer1_ref, head1_ref))):
        pooled = pooled_ref[:, tower * IN_WIDTH : (tower + 1) * IN_WIDTH]
        pre = dot(pooled, layer_ref[...])
        hidden = (pre * (1.0 / (1.0 + jnp.exp(-pre)))).astype(BF16)
        output = dot(hidden, head_ref[...])
        scale = lax.rsqrt(jnp.sum(output * output, axis=-1, keepdims=True) + EPSILON)
        unit = output * scale
        pre_ref[:, tower * HID : (tower + 1) * HID] = pre
        hidden_ref[:, tower * HID : (tower + 1) * HID] = hidden
        unit_ref[:, tower * OUT : (tower + 1) * OUT] = unit
        scale_ref[:, tower * OUT : (tower + 1) * OUT] = jnp.broadcast_to(scale, (OWN, OUT))
        rounded = unit.astype(BF16)
        for d in range(N_DP):
            send_ref[d, tower * OWN : (tower + 1) * OWN, :] = rounded
    counts = column_of(counts_ref[...].astype(F32))
    spread = jnp.broadcast_to(counts, (OWN, 128)).astype(BF16)
    for d in range(N_DP):
        send_ref[d, 2 * OWN : 3 * OWN, :] = spread


def towers(parts, counts, layer0, head0, layer1, head1):
    return pl.pallas_call(
        tower_kernel,
        in_specs=[whole()] * 6,
        out_specs=[whole()] * 6,
        out_shape=[
            jax.ShapeDtypeStruct((OWN, FEATURES * EMB), BF16),
            jax.ShapeDtypeStruct((OWN, 2 * HID), F32),
            jax.ShapeDtypeStruct((OWN, 2 * HID), BF16),
            jax.ShapeDtypeStruct((OWN, 2 * OUT), F32),
            jax.ShapeDtypeStruct((OWN, 2 * OUT), F32),
            jax.ShapeDtypeStruct((N_DP, 3 * OWN, 128), BF16),
        ],
        scratch_shapes=[pltpu.VMEM((BLOCK, EMB), F32)],
        compiler_params=room(8),
        name="towers",
    )(parts, counts, layer0, head0, layer1, head1)


def softmax_kernel(
    place_ref, group_ref, counts_ref, pooled_ref, pre_ref, hidden_ref, unit_ref, scale_ref,
    head0_ref, head1_ref, losses_ref, send_ref,
):
    size = N_DP * OWN
    group = group_ref[...]
    users = group[:, :OWN].reshape(size, OUT)
    items = group[:, OWN : 2 * OWN].reshape(size, OUT)
    log_freq = jnp.log(group[:, 2 * OWN :].reshape(size, 128).astype(F32))
    log_row = jnp.transpose(log_freq)[:1]
    own_log = jnp.log(column_of(counts_ref[...].astype(F32)))
    own_user = unit_ref[:, :OUT].astype(BF16)
    own_item = unit_ref[:, OUT:].astype(BF16)
    first = place_ref[1] * OWN
    mine = lax.broadcasted_iota(jnp.int32, (OWN, size), 1) == (
        lax.broadcasted_iota(jnp.int32, (OWN, size), 0) + first
    )
    down = INVERSE_TEMP * dot(items, users, NT) - jnp.concatenate([log_freq, log_freq], axis=1)
    lse_row = jnp.log(jnp.sum(jnp.exp(down), axis=0, keepdims=True))
    scores = INVERSE_TEMP * dot(own_user, items, NT) - log_row
    lse = jnp.log(jnp.sum(jnp.exp(scores), axis=1, keepdims=True))
    positive = jnp.sum(jnp.where(mine, scores, 0.0), axis=1, keepdims=True)
    losses_ref[...] = row_of(lse - positive)
    hot = mine.astype(F32)
    d_user = INVERSE_TEMP * dot((jnp.exp(scores - lse) - hot).astype(BF16), items)
    own_down = INVERSE_TEMP * dot(own_item, users, NT) - own_log
    d_item = INVERSE_TEMP * dot((jnp.exp(own_down - lse_row) - hot).astype(BF16), users)
    common = []
    outputs = []
    for tower, (d_unit, head_ref) in enumerate(((d_user, head0_ref), (d_item, head1_ref))):
        unit = unit_ref[:, tower * OUT : (tower + 1) * OUT]
        scale = scale_ref[:, tower * OUT : (tower + 1) * OUT]
        along = jnp.sum(unit * d_unit, axis=-1, keepdims=True)
        d_output = ((d_unit - unit * along) * scale).astype(BF16)
        pre = pre_ref[:, tower * HID : (tower + 1) * HID]
        gate = 1.0 / (1.0 + jnp.exp(-pre))
        slope = gate * (1.0 + pre * (1.0 - gate))
        common.append((dot(d_output, head_ref[...], NT) * slope).astype(BF16))
        outputs.append(d_output)
    common = jnp.concatenate(common + outputs, axis=1)
    pooled = pooled_ref[...]
    hidden = hidden_ref[...]
    blank = jnp.zeros((OWN, 64), BF16)
    for chip in range(N_CHIP):
        send_ref[chip, :, :COLUMNS_AT] = common
        send_ref[chip, :, COLUMNS_AT:] = jnp.concatenate(
            [
                pooled[:, chip * 64 : chip * 64 + 64],
                pooled[:, IN_WIDTH + chip * 64 : IN_WIDTH + chip * 64 + 64],
                hidden[:, chip * 32 : chip * 32 + 32],
                hidden[:, HID + chip * 32 : HID + chip * 32 + 32],
                blank,
            ],
            axis=1,
        )


def softmax_back(place, group, counts, pooled, pre, hidden, unit, scale, head0, head1):
    return pl.pallas_call(
        softmax_kernel,
        in_specs=[pl.BlockSpec(memory_space=pltpu.SMEM)] + [whole()] * 9,
        out_specs=[whole()] * 2,
        out_shape=[
            jax.ShapeDtypeStruct((1, OWN), F32),
            jax.ShapeDtypeStruct((N_CHIP, OWN, GRAD_WIDTH), BF16),
        ],
        compiler_params=room(6),
        name="softmax_back",
    )(place, group, counts, pooled, pre, hidden, unit, scale, head0, head1)


def back_kernel(first, spans, *refs):
    place_ref, grads_ref, layer0_ref, layer1_ref = refs[:4]
    weights_refs = refs[4 : 4 + len(spans)]
    refs = refs[4 + len(spans) :]
    if first:
        total_ref, layers_ref, heads_ref, pooled_ref = refs
    else:
        before_ref, layers_before_ref, heads_before_ref = refs[:3]
        send_ref, pooled_ref, layers_ref, heads_ref = refs[3:]
    samples = N_CHIP * OWN
    half = samples * FEATURES // 2
    grads = grads_ref[...].reshape(samples, GRAD_WIDTH)
    inputs = grads[:, COLUMNS_AT : COLUMNS_AT + 128]
    hidden = grads[:, COLUMNS_AT + 128 :]
    d_hidden = (grads[:, :HID], grads[:, HID : 2 * HID])
    for f in range(FEATURES):
        tower = f // TOWER_FEATURES
        layer_ref = (layer0_ref, layer1_ref)[tower]
        at = (f % TOWER_FEATURES) * EMB
        pooled_ref[pl.ds(f, samples, stride=FEATURES), :] = dot(
            d_hidden[tower], layer_ref[at : at + EMB, :], NT
        )
    for tower in range(2):
        d_output = grads[:, 2 * HID + tower * OUT : 2 * HID + (tower + 1) * OUT]
        layer_rows = dot(inputs, d_hidden[tower], TN)[tower * 64 : tower * 64 + 64]
        head_rows = dot(hidden, d_output, TN)[tower * 32 : tower * 32 + 32]
        if not first:
            layer_rows = layer_rows + layers_before_ref[tower]
            head_rows = head_rows + heads_before_ref[tower]
        layers_ref[tower] = layer_rows
        heads_ref[tower] = head_rows
    total = None if first else before_ref[...]
    for groups, weights_ref in zip(spans, weights_refs):
        here = 0
        for other_x, low, high in groups:
            first_row = (place_ref[2] ^ other_x) * half
            for start in range(low * BLOCK, high * BLOCK, BACK_ROWS):
                at = pl.ds(pl.multiple_of(first_row + start, BACK_ROWS), BACK_ROWS)
                weights = weights_ref[here : here + BACK_ROWS, :]
                term = dot(pooled_ref[at, :].astype(BF16), weights, TN)
                total = term if total is None else total + term
                here += BACK_ROWS
    if first:
        total_ref[...] = total
        return
    table_rows = jnp.transpose(total)
    core = place_ref[0]
    for d in range(N_DP):
        send_ref[d, :64, :] = table_rows[d * 64 : (d + 1) * 64].astype(BF16)
        tower, quarter, half = d // 8, d % 8 // 2, d % 2
        send_ref[d, 64:80, :] = layers_ref[
            tower,
            pl.ds(pl.multiple_of(core * 32 + half * 16, 16), 16),
            quarter * 128 : quarter * 128 + 128,
        ].astype(BF16)
        if d < 4:
            at = pl.multiple_of(core * 16 + d % 2 * 8, 8)
            send_ref[d, 80:, :] = heads_ref[d // 2, pl.ds(at, 8), :].astype(BF16)
        else:
            send_ref[d, 80:, :] = jnp.zeros((8, 128), BF16)


def back(place, grads, weights, layer0, layer1, before=None):
    first = before is None
    spans = tuple(weights)
    total = jax.ShapeDtypeStruct((EMB, ROWS), F32)
    layers = jax.ShapeDtypeStruct((2, 64, HID), F32)
    heads = jax.ShapeDtypeStruct((2, 32, OUT), F32)
    scratch = [pltpu.VMEM((N_CHIP * BLOCK, EMB), F32)]
    if first:
        out_shape = [total, layers, heads]
    else:
        out_shape = [jax.ShapeDtypeStruct((N_DP, CHUNK, 128), BF16)]
        scratch += [pltpu.VMEM(layers.shape, F32), pltpu.VMEM(heads.shape, F32)]
    before = before or ()
    return pl.pallas_call(
        lambda *refs: back_kernel(first, spans, *refs),
        in_specs=[
            pl.BlockSpec(memory_space=pltpu.SMEM),
        ]
        + [whole()] * (3 + len(spans) + len(before)),
        out_specs=[whole()] * len(out_shape),
        out_shape=out_shape,
        scratch_shapes=scratch,
        compiler_params=room(12),
        cost_estimate=pl.CostEstimate(
            flops=2 * N_CHIP * BLOCK * ROWS * EMB, bytes_accessed=10 * 2**20, transcendentals=0
        ),
        name="back",
    )(place, grads, layer0, layer1, *weights.values(), *before)


def sum_kernel(parts_ref, send_ref):
    total = parts_ref[0].astype(F32)
    for d in range(1, N_DP):
        total = total + parts_ref[d].astype(F32)
    total = total.astype(BF16)
    for d in range(N_DP):
        send_ref[d] = total


def sum_parts(parts):
    return pl.pallas_call(
        sum_kernel,
        in_specs=[whole()],
        out_specs=whole(),
        out_shape=jax.ShapeDtypeStruct(parts.shape, BF16),
        compiler_params=room(2),
        name="sum_parts",
    )(parts)


def spread_kernel(sums_ref, table_ref, layer0_ref, head0_ref, layer1_ref, head1_ref):
    for d in range(N_DP):
        table_ref[d * 64 : (d + 1) * 64, :] = sums_ref[d, :64, :].astype(F32)
        tower, quarter, half = d // 8, d % 8 // 2, d % 2
        (layer0_ref, layer1_ref)[tower][
            half * 16 : half * 16 + 16, quarter * 128 : quarter * 128 + 128
        ] = sums_ref[d, 64:80, :].astype(F32)
    for d in range(4):
        (head0_ref, head1_ref)[d // 2][d % 2 * 8 : d % 2 * 8 + 8, :] = sums_ref[d, 80:, :].astype(F32)


def spread(sums):
    return pl.pallas_call(
        spread_kernel,
        in_specs=[whole()],
        out_specs=[whole()] * 5,
        out_shape=[
            jax.ShapeDtypeStruct((ROWS, EMB), F32),
            jax.ShapeDtypeStruct((32, HID), F32),
            jax.ShapeDtypeStruct((16, OUT), F32),
            jax.ShapeDtypeStruct((32, HID), F32),
            jax.ShapeDtypeStruct((16, OUT), F32),
        ],
        compiler_params=room(4),
        name="spread",
    )(sums)


def exchange(values, axes):
    return lax.all_to_all(values, axes, 0, 0, tiled=True)


def to_other(values, axis):
    return lax.ppermute(values, axis, [(0, 1), (1, 0)])


def add(*terms):
    return sum(term.astype(F32) for term in terms).astype(BF16)


def shards(ids, mults, table, user_layer, user_head, item_layer, item_head, counts):
    place = jnp.stack([lax.axis_index("core"), lax.axis_index(DP), lax.axis_index("x_lo")])
    lookups = ids[0] + 1024 * mults[0]
    half = N_Z // 2 * BLOCK
    whole_x = N_Z * BLOCK
    both = ((1, 0, N_Z), (0, 0, N_Z))
    low, high, own = ((1, 0, N_Z // 2),), ((1, N_Z // 2, N_Z),), ((0, 0, N_Z),)
    core_weights, core_partial = pool(both, 1, place, lookups, table)
    core_arrived = to_other(core_partial, "core")
    low_weights, low_partial = pool(low, 0, place, lookups, table)
    low_sum, lookups = lax.optimization_barrier((add(low_partial, core_arrived[:half]), lookups))
    low_arrived = to_other(low_sum, "x_lo")
    high_weights, high_partial = pool(high, 0, place, lookups, table)
    high_sum, lookups = lax.optimization_barrier(
        (add(high_partial, core_arrived[half:whole_x]), lookups)
    )
    high_arrived = to_other(high_sum, "x_lo")
    own_weights, own_partial = pool(own, 0, place, lookups, table)
    x_arrived = jnp.concatenate([low_arrived, high_arrived])
    total_partial = add(own_partial, core_arrived[whole_x:], x_arrived)
    parts = exchange(total_partial.reshape(N_Z, BLOCK, EMB), "z")
    pooled, pre, hidden, unit, scale, units = towers(
        parts, counts, user_layer, user_head, item_layer, item_head
    )
    group = exchange(units, DP)
    losses, grads = softmax_back(
        place, group, counts, pooled, pre, hidden, unit, scale, user_head, item_head
    )
    own_grads = exchange(grads, CHIPS)
    other_grads = to_other(own_grads, "core")
    weights = {own: own_weights, low: low_weights, high: high_weights}
    before = back(place, own_grads, weights, user_layer, item_layer)
    (terms,) = back(
        place, other_grads, {both: core_weights}, user_layer, item_layer, tuple(before)
    )
    sums = exchange(sum_parts(exchange(terms, DP)), DP)
    table_change, layer0, head0, layer1, head1 = spread(sums)
    return (losses, table_change, layer0, head0, layer1, head1)


def solution(mesh):
    fine = Mesh(mesh.devices.reshape(tuple(AXES.values())), tuple(AXES))
    in_specs = (
        P(TABLE, DP, None),
        P(TABLE, DP, None),
        P(TABLE, None),
        P(),
        P(),
        P(),
        P(),
        P(DP, TABLE),
    )
    out_specs = (P(DP, TABLE),) + (P(TABLE, None),) * 5
    return jax.shard_map(shards, mesh=fine, in_specs=in_specs, out_specs=out_specs, check_vma=False)
```

```python
import jax
import jax.numpy as jnp
from jax import lax
from jax.experimental import pallas as pl
from jax.experimental.pallas import tpu as pltpu
from jax.sharding import Mesh
from jax.sharding import PartitionSpec as P

LOOKUPS = 8
INVERSE_TEMP = 20.0
EPSILON = 1e-06

AXES = {"x_lo": 2, "z": 8, "core": 2, "x_hi": 2, "y": 8}
TABLE = ("x_lo", "z", "core")
CHIPS = ("x_lo", "z")
DP = ("x_hi", "y")
N_CHIP = 16
N_Z = 8
N_DP = 16
OWN = 16
FEATURES = 16
TOWER_FEATURES = 8
ROWS = 1024
EMB = 128
HID = 512
OUT = 128
BLOCK = OWN * FEATURES
IN_WIDTH = TOWER_FEATURES * EMB
GRAD_WIDTH = 12 * 128
COLUMNS_AT = 2 * HID + 2 * OUT
POOL_SAMPLES = 32
BACK_PARTS = 2
CHUNK = 88

BF16 = jnp.bfloat16
F32 = jnp.float32

NT = (((1,), (1,)), ((), ()))
TN = (((0,), (0,)), ((), ()))


def dot(left, right, dims=(((1,), (0,)), ((), ()))):
    return lax.dot_general(left, right, dims, preferred_element_type=F32)


def room(mib):
    return pltpu.CompilerParams(vmem_limit_bytes=mib * 2**20)


def whole():
    return pl.BlockSpec(memory_space=pltpu.VMEM)


def lookup_weights(ids, mults, weights_ref, first):
    lane = lax.broadcasted_iota(jnp.int32, ids.shape, 1)
    high = lax.shift_right_logical(ids, 7) * FEATURES + lax.shift_right_logical(lane, 3)
    high = high.astype(F32)
    low = jnp.transpose((ids & 127).astype(F32))
    mults = mults.astype(F32)
    down = lax.broadcasted_iota(jnp.int32, (128, 128), 0).astype(F32).astype(BF16)
    across = lax.broadcasted_iota(jnp.int32, (128, 128), 1).astype(F32).astype(BF16)
    zero = jnp.zeros((128, 128), BF16)
    one = jnp.ones((128, 128), BF16)

    def spread_row(values, n):
        row = jnp.broadcast_to(values[n : n + 1], (16, 128)).astype(BF16)
        return jnp.concatenate([row] * 8, axis=0)

    for n in range(ids.shape[0]):
        left = jnp.where(spread_row(high, n) == down, spread_row(mults, n), zero)
        spread_low = jnp.broadcast_to(low[:, n : n + 1], (128, 128)).astype(BF16)
        right = jnp.where(spread_low == across, one, zero)
        hits = dot(left, right).astype(BF16)
        at = first + n * FEATURES
        for h in range(8):
            weights_ref[at : at + FEATURES, h * 128 : (h + 1) * 128] = hits[
                h * FEATURES : (h + 1) * FEATURES
            ]


def pool_kernel(other_x, other_core, place_ref, lookups_ref, table_ref, weights_ref, partial_ref):
    core = place_ref[0] ^ other_core
    x_lo = place_ref[2] ^ other_x
    parts = N_Z * OWN // POOL_SAMPLES
    rows = POOL_SAMPLES * FEATURES

    def sum_part(part):
        at = pl.ds(part * rows, rows)
        partial_ref[at, :] = dot(weights_ref[at, :], table_ref[...]).astype(BF16)

    for part in range(parts):
        chips = range(part * POOL_SAMPLES // OWN, (part + 1) * POOL_SAMPLES // OWN)
        starts = [pl.multiple_of((2 * (x_lo * N_Z + z) + core) * OWN, OWN) for z in chips]
        lookups = jnp.concatenate([lookups_ref[pl.ds(start, OWN), :] for start in starts], axis=0)
        lookup_weights(lookups & 1023, lax.shift_right_logical(lookups, 10), weights_ref, part * rows)
        if part > 0:
            sum_part(part - 1)
    sum_part(parts - 1)


def pool(other_x, other_core, place, lookups, table):
    return pl.pallas_call(
        lambda *refs: pool_kernel(other_x, other_core, *refs),
        in_specs=[pl.BlockSpec(memory_space=pltpu.SMEM)] + [whole()] * 2,
        out_specs=[whole()] * 2,
        out_shape=[
            jax.ShapeDtypeStruct((N_Z * BLOCK, ROWS), BF16),
            jax.ShapeDtypeStruct((N_Z * BLOCK, EMB), BF16),
        ],
        compiler_params=room(8),
        cost_estimate=pl.CostEstimate(
            flops=2 * N_Z * BLOCK * ROWS * EMB * 2, bytes_accessed=5 * 2**20, transcendentals=0
        ),
        name="pool",
    )(place, lookups, table)


def column_of(row):
    eye = lax.broadcasted_iota(jnp.int32, (OWN, OWN), 0) == lax.broadcasted_iota(
        jnp.int32, (OWN, OWN), 1
    )
    return jnp.sum(jnp.where(eye, row, 0.0), axis=1, keepdims=True)


def row_of(column):
    eye = lax.broadcasted_iota(jnp.int32, (OWN, OWN), 0) == lax.broadcasted_iota(
        jnp.int32, (OWN, OWN), 1
    )
    return jnp.sum(jnp.where(eye, column, 0.0), axis=0, keepdims=True)


def tower_kernel(
    parts_ref, counts_ref, layer0_ref, head0_ref, layer1_ref, head1_ref,
    pooled_ref, pre_ref, hidden_ref, unit_ref, scale_ref, send_ref, rows_ref,
):
    total = parts_ref[0].astype(F32)
    for s in range(1, N_Z):
        total = total + parts_ref[s].astype(F32)
    rows_ref[:BLOCK, :] = total
    for f in range(FEATURES):
        pooled_ref[:, f * EMB : (f + 1) * EMB] = rows_ref[
            pl.ds(f, OWN, stride=FEATURES), :
        ].astype(BF16)
    for tower, (layer_ref, head_ref) in enumerate(((layer0_ref, head0_ref), (layer1_ref, head1_ref))):
        pooled = pooled_ref[:, tower * IN_WIDTH : (tower + 1) * IN_WIDTH]
        pre = dot(pooled, layer_ref[...])
        hidden = (pre * (1.0 / (1.0 + jnp.exp(-pre)))).astype(BF16)
        output = dot(hidden, head_ref[...])
        scale = lax.rsqrt(jnp.sum(output * output, axis=-1, keepdims=True) + EPSILON)
        unit = output * scale
        pre_ref[:, tower * HID : (tower + 1) * HID] = pre
        hidden_ref[:, tower * HID : (tower + 1) * HID] = hidden
        unit_ref[:, tower * OUT : (tower + 1) * OUT] = unit
        scale_ref[:, tower * OUT : (tower + 1) * OUT] = jnp.broadcast_to(scale, (OWN, OUT))
        rounded = unit.astype(BF16)
        for d in range(N_DP):
            send_ref[d, tower * OWN : (tower + 1) * OWN, :] = rounded
    counts = column_of(counts_ref[...].astype(F32))
    spread = jnp.broadcast_to(counts, (OWN, 128)).astype(BF16)
    for d in range(N_DP):
        send_ref[d, 2 * OWN : 3 * OWN, :] = spread


def towers(parts, counts, layer0, head0, layer1, head1):
    return pl.pallas_call(
        tower_kernel,
        in_specs=[whole()] * 6,
        out_specs=[whole()] * 6,
        out_shape=[
            jax.ShapeDtypeStruct((OWN, FEATURES * EMB), BF16),
            jax.ShapeDtypeStruct((OWN, 2 * HID), F32),
            jax.ShapeDtypeStruct((OWN, 2 * HID), BF16),
            jax.ShapeDtypeStruct((OWN, 2 * OUT), F32),
            jax.ShapeDtypeStruct((OWN, 2 * OUT), F32),
            jax.ShapeDtypeStruct((N_DP, 3 * OWN, 128), BF16),
        ],
        scratch_shapes=[pltpu.VMEM((BLOCK + FEATURES, EMB), F32)],
        compiler_params=room(8),
        name="towers",
    )(parts, counts, layer0, head0, layer1, head1)


def softmax_kernel(
    place_ref, group_ref, counts_ref, pooled_ref, pre_ref, hidden_ref, unit_ref, scale_ref,
    head0_ref, head1_ref, losses_ref, send_ref,
):
    size = N_DP * OWN
    group = group_ref[...]
    users = group[:, :OWN].reshape(size, OUT)
    items = group[:, OWN : 2 * OWN].reshape(size, OUT)
    log_freq = jnp.log(group[:, 2 * OWN :].reshape(size, 128).astype(F32))
    log_row = jnp.transpose(log_freq)[:1]
    own_log = jnp.log(column_of(counts_ref[...].astype(F32)))
    own_user = unit_ref[:, :OUT].astype(BF16)
    own_item = unit_ref[:, OUT:].astype(BF16)
    first = place_ref[1] * OWN
    mine = lax.broadcasted_iota(jnp.int32, (OWN, size), 1) == (
        lax.broadcasted_iota(jnp.int32, (OWN, size), 0) + first
    )
    down = INVERSE_TEMP * dot(items, users, NT) - jnp.concatenate([log_freq, log_freq], axis=1)
    lse_row = jnp.log(jnp.sum(jnp.exp(down), axis=0, keepdims=True))
    scores = INVERSE_TEMP * dot(own_user, items, NT) - log_row
    lse = jnp.log(jnp.sum(jnp.exp(scores), axis=1, keepdims=True))
    positive = jnp.sum(jnp.where(mine, scores, 0.0), axis=1, keepdims=True)
    losses_ref[...] = row_of(lse - positive)
    hot = mine.astype(F32)
    d_user = INVERSE_TEMP * dot((jnp.exp(scores - lse) - hot).astype(BF16), items)
    own_down = INVERSE_TEMP * dot(own_item, users, NT) - own_log
    d_item = INVERSE_TEMP * dot((jnp.exp(own_down - lse_row) - hot).astype(BF16), users)
    common = []
    outputs = []
    for tower, (d_unit, head_ref) in enumerate(((d_user, head0_ref), (d_item, head1_ref))):
        unit = unit_ref[:, tower * OUT : (tower + 1) * OUT]
        scale = scale_ref[:, tower * OUT : (tower + 1) * OUT]
        along = jnp.sum(unit * d_unit, axis=-1, keepdims=True)
        d_output = ((d_unit - unit * along) * scale).astype(BF16)
        pre = pre_ref[:, tower * HID : (tower + 1) * HID]
        gate = 1.0 / (1.0 + jnp.exp(-pre))
        slope = gate * (1.0 + pre * (1.0 - gate))
        common.append((dot(d_output, head_ref[...], NT) * slope).astype(BF16))
        outputs.append(d_output)
    common = jnp.concatenate(common + outputs, axis=1)
    pooled = pooled_ref[...]
    hidden = hidden_ref[...]
    blank = jnp.zeros((OWN, 64), BF16)
    for chip in range(N_CHIP):
        send_ref[chip, :, :COLUMNS_AT] = common
        send_ref[chip, :, COLUMNS_AT:] = jnp.concatenate(
            [
                pooled[:, chip * 64 : chip * 64 + 64],
                pooled[:, IN_WIDTH + chip * 64 : IN_WIDTH + chip * 64 + 64],
                hidden[:, chip * 32 : chip * 32 + 32],
                hidden[:, HID + chip * 32 : HID + chip * 32 + 32],
                blank,
            ],
            axis=1,
        )


def softmax_back(place, group, counts, pooled, pre, hidden, unit, scale, head0, head1):
    return pl.pallas_call(
        softmax_kernel,
        in_specs=[pl.BlockSpec(memory_space=pltpu.SMEM)] + [whole()] * 9,
        out_specs=[whole()] * 2,
        out_shape=[
            jax.ShapeDtypeStruct((1, OWN), F32),
            jax.ShapeDtypeStruct((N_CHIP, OWN, GRAD_WIDTH), BF16),
        ],
        compiler_params=room(6),
        name="softmax_back",
    )(place, group, counts, pooled, pre, hidden, unit, scale, head0, head1)


def back_kernel(first, *refs):
    place_ref, grads_ref, here_ref, there_ref, layer0_ref, layer1_ref = refs[:6]
    if first:
        total_ref, layers_ref, heads_ref, pooled_ref = refs[6:]
    else:
        before_ref, layers_before_ref, heads_before_ref = refs[6:9]
        send_ref, pooled_ref, layers_ref, heads_ref = refs[9:]
    samples = N_CHIP * OWN
    half = samples * FEATURES // 2
    rows = half // BACK_PARTS
    grads = grads_ref[...].reshape(samples, GRAD_WIDTH)
    inputs = grads[:, COLUMNS_AT : COLUMNS_AT + 128]
    hidden = grads[:, COLUMNS_AT + 128 :]
    d_hidden = (grads[:, :HID], grads[:, HID : 2 * HID])
    for f in range(FEATURES):
        tower = f // TOWER_FEATURES
        layer_ref = (layer0_ref, layer1_ref)[tower]
        at = (f % TOWER_FEATURES) * EMB
        pooled_ref[pl.ds(f, samples, stride=FEATURES), :] = dot(
            d_hidden[tower], layer_ref[at : at + EMB, :], NT
        )
    for tower in range(2):
        d_output = grads[:, 2 * HID + tower * OUT : 2 * HID + (tower + 1) * OUT]
        layer_rows = dot(inputs, d_hidden[tower], TN)[tower * 64 : tower * 64 + 64]
        head_rows = dot(hidden, d_output, TN)[tower * 32 : tower * 32 + 32]
        if not first:
            layer_rows = layer_rows + layers_before_ref[tower]
            head_rows = head_rows + heads_before_ref[tower]
        layers_ref[tower] = layer_rows
        heads_ref[tower] = head_rows
    total = None if first else before_ref[...]
    for other_x, weights_ref in enumerate((here_ref, there_ref)):
        first_row = (place_ref[2] ^ other_x) * half
        for part in range(BACK_PARTS):
            at = pl.ds(pl.multiple_of(first_row + part * rows, rows), rows)
            weights = weights_ref[part * rows : (part + 1) * rows, :]
            term = dot(pooled_ref[at, :].astype(BF16), weights, TN)
            total = term if total is None else total + term
    if first:
        total_ref[...] = total
        return
    table_rows = jnp.transpose(total)
    core = place_ref[0]
    for d in range(N_DP):
        send_ref[d, :64, :] = table_rows[d * 64 : (d + 1) * 64].astype(BF16)
        tower, quarter, half = d // 8, d % 8 // 2, d % 2
        send_ref[d, 64:80, :] = layers_ref[
            tower,
            pl.ds(pl.multiple_of(core * 32 + half * 16, 16), 16),
            quarter * 128 : quarter * 128 + 128,
        ].astype(BF16)
        if d < 4:
            at = pl.multiple_of(core * 16 + d % 2 * 8, 8)
            send_ref[d, 80:, :] = heads_ref[d // 2, pl.ds(at, 8), :].astype(BF16)
        else:
            send_ref[d, 80:, :] = jnp.zeros((8, 128), BF16)


def back(place, grads, weights, layer0, layer1, before=None):
    first = before is None
    total = jax.ShapeDtypeStruct((EMB, ROWS), F32)
    layers = jax.ShapeDtypeStruct((2, 64, HID), F32)
    heads = jax.ShapeDtypeStruct((2, 32, OUT), F32)
    scratch = [pltpu.VMEM((N_CHIP * BLOCK + FEATURES, EMB), F32)]
    if first:
        out_shape = [total, layers, heads]
    else:
        out_shape = [jax.ShapeDtypeStruct((N_DP, CHUNK, 128), BF16)]
        scratch += [pltpu.VMEM(layers.shape, F32), pltpu.VMEM(heads.shape, F32)]
    before = before or ()
    return pl.pallas_call(
        lambda *refs: back_kernel(first, *refs),
        in_specs=[
            pl.BlockSpec(memory_space=pltpu.SMEM),
        ]
        + [whole()] * (5 + len(before)),
        out_specs=[whole()] * len(out_shape),
        out_shape=out_shape,
        scratch_shapes=scratch,
        compiler_params=room(12),
        cost_estimate=pl.CostEstimate(
            flops=2 * N_CHIP * BLOCK * ROWS * EMB, bytes_accessed=10 * 2**20, transcendentals=0
        ),
        name="back",
    )(place, grads, *weights, layer0, layer1, *before)


def sum_kernel(parts_ref, send_ref):
    total = parts_ref[0].astype(F32)
    for d in range(1, N_DP):
        total = total + parts_ref[d].astype(F32)
    total = total.astype(BF16)
    for d in range(N_DP):
        send_ref[d] = total


def sum_parts(parts):
    return pl.pallas_call(
        sum_kernel,
        in_specs=[whole()],
        out_specs=whole(),
        out_shape=jax.ShapeDtypeStruct(parts.shape, BF16),
        compiler_params=room(2),
        name="sum_parts",
    )(parts)


def spread_kernel(sums_ref, table_ref, layer0_ref, head0_ref, layer1_ref, head1_ref):
    for d in range(N_DP):
        table_ref[d * 64 : (d + 1) * 64, :] = sums_ref[d, :64, :].astype(F32)
        tower, quarter, half = d // 8, d % 8 // 2, d % 2
        (layer0_ref, layer1_ref)[tower][
            half * 16 : half * 16 + 16, quarter * 128 : quarter * 128 + 128
        ] = sums_ref[d, 64:80, :].astype(F32)
    for d in range(4):
        (head0_ref, head1_ref)[d // 2][d % 2 * 8 : d % 2 * 8 + 8, :] = sums_ref[d, 80:, :].astype(F32)


def spread(sums):
    return pl.pallas_call(
        spread_kernel,
        in_specs=[whole()],
        out_specs=[whole()] * 5,
        out_shape=[
            jax.ShapeDtypeStruct((ROWS, EMB), F32),
            jax.ShapeDtypeStruct((32, HID), F32),
            jax.ShapeDtypeStruct((16, OUT), F32),
            jax.ShapeDtypeStruct((32, HID), F32),
            jax.ShapeDtypeStruct((16, OUT), F32),
        ],
        compiler_params=room(4),
        name="spread",
    )(sums)


def exchange(values, axes):
    return lax.all_to_all(values, axes, 0, 0, tiled=True)


def to_other(values, axis):
    return lax.ppermute(values, axis, [(0, 1), (1, 0)])


def add(*terms):
    return sum(term.astype(F32) for term in terms).astype(BF16)


def shards(ids, mults, table, user_layer, user_head, item_layer, item_head, counts):
    place = jnp.stack([lax.axis_index("core"), lax.axis_index(DP), lax.axis_index("x_lo")])
    lookups = ids[0] + 1024 * mults[0]
    both_weights, both_partial = pool(1, 1, place, lookups, table)
    both_arrived = to_other(both_partial, "core")
    x_weights, x_partial = pool(1, 0, place, lookups, table)
    x_sum, lookups = lax.optimization_barrier((add(x_partial, both_arrived), lookups))
    x_arrived = to_other(x_sum, "x_lo")
    core_weights, core_partial = pool(0, 1, place, lookups, table)
    core_arrived = to_other(core_partial, "core")
    own_weights, own_partial = pool(0, 0, place, lookups, table)
    total_partial = add(own_partial, core_arrived, x_arrived)
    parts = exchange(total_partial.reshape(N_Z, BLOCK, EMB), "z")
    pooled, pre, hidden, unit, scale, units = towers(
        parts, counts, user_layer, user_head, item_layer, item_head
    )
    group = exchange(units, DP)
    losses, grads = softmax_back(
        place, group, counts, pooled, pre, hidden, unit, scale, user_head, item_head
    )
    own_grads = exchange(grads, CHIPS)
    other_grads = to_other(own_grads, "core")
    before = back(place, own_grads, (own_weights, x_weights), user_layer, item_layer)
    (terms,) = back(
        place, other_grads, (core_weights, both_weights), user_layer, item_layer, tuple(before)
    )
    sums = exchange(sum_parts(exchange(terms, DP)), DP)
    table_change, layer0, head0, layer1, head1 = spread(sums)
    return (losses, table_change, layer0, head0, layer1, head1)


def solution(mesh):
    fine = Mesh(mesh.devices.reshape(tuple(AXES.values())), tuple(AXES))
    in_specs = (
        P(TABLE, DP, None),
        P(TABLE, DP, None),
        P(TABLE, None),
        P(),
        P(),
        P(),
        P(),
        P(DP, TABLE),
    )
    out_specs = (P(DP, TABLE),) + (P(TABLE, None),) * 5
    return jax.shard_map(shards, mesh=fine, in_specs=in_specs, out_specs=out_specs, check_vma=False)
```

```python
import jax
import jax.numpy as jnp
from jax import lax
from jax.experimental import pallas as pl
from jax.experimental.pallas import tpu as pltpu
from jax.sharding import Mesh
from jax.sharding import PartitionSpec as P

LOOKUPS = 8
INVERSE_TEMP = 20.0
EPSILON = 1e-06

AXES = {"x_lo": 2, "z": 8, "core": 2, "x_hi": 2, "y": 8}
TABLE = ("x_lo", "z", "core")
CHIPS = ("x_lo", "z")
DP = ("x_hi", "y")
N_CHIP = 16
N_Z = 8
N_DP = 16
OWN = 16
FEATURES = 16
TOWER_FEATURES = 8
ROWS = 1024
EMB = 128
HID = 512
OUT = 128
BLOCK = OWN * FEATURES
IN_WIDTH = TOWER_FEATURES * EMB
GRAD_WIDTH = 12 * 128
COLUMNS_AT = 2 * HID + 2 * OUT
POOL_SAMPLES = 32
BACK_PARTS = 2
CHUNK = 88

BF16 = jnp.bfloat16
F32 = jnp.float32

NT = (((1,), (1,)), ((), ()))
TN = (((0,), (0,)), ((), ()))


def dot(left, right, dims=(((1,), (0,)), ((), ()))):
    return lax.dot_general(left, right, dims, preferred_element_type=F32)


def room(mib):
    return pltpu.CompilerParams(vmem_limit_bytes=mib * 2**20)


def whole():
    return pl.BlockSpec(memory_space=pltpu.VMEM)


def lookup_weights(ids, mults, weights_ref, first):
    lane = lax.broadcasted_iota(jnp.int32, ids.shape, 1)
    high = lax.shift_right_logical(ids, 7) * FEATURES + lax.shift_right_logical(lane, 3)
    high = high.astype(F32)
    low = jnp.transpose((ids & 127).astype(F32))
    mults = mults.astype(F32)
    down = lax.broadcasted_iota(jnp.int32, (128, 128), 0).astype(F32).astype(BF16)
    across = lax.broadcasted_iota(jnp.int32, (128, 128), 1).astype(F32).astype(BF16)
    zero = jnp.zeros((128, 128), BF16)
    one = jnp.ones((128, 128), BF16)

    def spread_row(values, n):
        row = jnp.broadcast_to(values[n : n + 1], (16, 128)).astype(BF16)
        return jnp.concatenate([row] * 8, axis=0)

    for n in range(ids.shape[0]):
        left = jnp.where(spread_row(high, n) == down, spread_row(mults, n), zero)
        spread_low = jnp.broadcast_to(low[:, n : n + 1], (128, 128)).astype(BF16)
        right = jnp.where(spread_low == across, one, zero)
        hits = dot(left, right).astype(BF16)
        at = first + n * FEATURES
        for h in range(8):
            weights_ref[at : at + FEATURES, h * 128 : (h + 1) * 128] = hits[
                h * FEATURES : (h + 1) * FEATURES
            ]


def pool_kernel(other_x, other_core, place_ref, lookups_ref, table_ref, weights_ref, partial_ref):
    core = place_ref[0] ^ other_core
    x_lo = place_ref[2] ^ other_x
    parts = N_Z * OWN // POOL_SAMPLES
    rows = POOL_SAMPLES * FEATURES

    def sum_part(part):
        at = pl.ds(part * rows, rows)
        partial_ref[at, :] = dot(weights_ref[at, :], table_ref[...]).astype(BF16)

    for part in range(parts):
        chips = range(part * POOL_SAMPLES // OWN, (part + 1) * POOL_SAMPLES // OWN)
        starts = [pl.multiple_of((2 * (x_lo * N_Z + z) + core) * OWN, OWN) for z in chips]
        lookups = jnp.concatenate([lookups_ref[pl.ds(start, OWN), :] for start in starts], axis=0)
        lookup_weights(lookups & 1023, lax.shift_right_logical(lookups, 10), weights_ref, part * rows)
        if part > 0:
            sum_part(part - 1)
    sum_part(parts - 1)


def pool(other_x, other_core, place, lookups, table):
    return pl.pallas_call(
        lambda *refs: pool_kernel(other_x, other_core, *refs),
        in_specs=[pl.BlockSpec(memory_space=pltpu.SMEM)] + [whole()] * 2,
        out_specs=[whole()] * 2,
        out_shape=[
            jax.ShapeDtypeStruct((N_Z * BLOCK, ROWS), BF16),
            jax.ShapeDtypeStruct((N_Z * BLOCK, EMB), BF16),
        ],
        compiler_params=room(8),
        cost_estimate=pl.CostEstimate(
            flops=2 * N_Z * BLOCK * ROWS * EMB * 2, bytes_accessed=5 * 2**20, transcendentals=0
        ),
        name="pool",
    )(place, lookups, table)


def column_of(row):
    eye = lax.broadcasted_iota(jnp.int32, (OWN, OWN), 0) == lax.broadcasted_iota(
        jnp.int32, (OWN, OWN), 1
    )
    return jnp.sum(jnp.where(eye, row, 0.0), axis=1, keepdims=True)


def row_of(column):
    eye = lax.broadcasted_iota(jnp.int32, (OWN, OWN), 0) == lax.broadcasted_iota(
        jnp.int32, (OWN, OWN), 1
    )
    return jnp.sum(jnp.where(eye, column, 0.0), axis=0, keepdims=True)


def tower_kernel(
    parts_ref, counts_ref, layer0_ref, head0_ref, layer1_ref, head1_ref,
    pooled_ref, pre_ref, hidden_ref, unit_ref, scale_ref, send_ref, rows_ref,
):
    total = parts_ref[0].astype(F32)
    for s in range(1, N_Z):
        total = total + parts_ref[s].astype(F32)
    rows_ref[:BLOCK, :] = total
    for f in range(FEATURES):
        pooled_ref[:, f * EMB : (f + 1) * EMB] = rows_ref[
            pl.ds(f, OWN, stride=FEATURES), :
        ].astype(BF16)
    for tower, (layer_ref, head_ref) in enumerate(((layer0_ref, head0_ref), (layer1_ref, head1_ref))):
        pooled = pooled_ref[:, tower * IN_WIDTH : (tower + 1) * IN_WIDTH]
        pre = dot(pooled, layer_ref[...])
        hidden = (pre * (1.0 / (1.0 + jnp.exp(-pre)))).astype(BF16)
        output = dot(hidden, head_ref[...])
        scale = lax.rsqrt(jnp.sum(output * output, axis=-1, keepdims=True) + EPSILON)
        unit = output * scale
        pre_ref[:, tower * HID : (tower + 1) * HID] = pre
        hidden_ref[:, tower * HID : (tower + 1) * HID] = hidden
        unit_ref[:, tower * OUT : (tower + 1) * OUT] = unit
        scale_ref[:, tower * OUT : (tower + 1) * OUT] = jnp.broadcast_to(scale, (OWN, OUT))
        rounded = unit.astype(BF16)
        for d in range(N_DP):
            send_ref[d, tower * OWN : (tower + 1) * OWN, :] = rounded
    counts = column_of(counts_ref[...].astype(F32))
    spread = jnp.broadcast_to(counts, (OWN, 128))
    left = lax.broadcasted_iota(jnp.int32, (OWN // 2, 128), 1) < 64
    spread = jnp.where(left, spread[: OWN // 2], spread[OWN // 2 :]).astype(BF16)
    for d in range(N_DP):
        send_ref[d, 2 * OWN :, :] = spread


def towers(parts, counts, layer0, head0, layer1, head1):
    return pl.pallas_call(
        tower_kernel,
        in_specs=[whole()] * 6,
        out_specs=[whole()] * 6,
        out_shape=[
            jax.ShapeDtypeStruct((OWN, FEATURES * EMB), BF16),
            jax.ShapeDtypeStruct((OWN, 2 * HID), F32),
            jax.ShapeDtypeStruct((OWN, 2 * HID), BF16),
            jax.ShapeDtypeStruct((OWN, 2 * OUT), F32),
            jax.ShapeDtypeStruct((OWN, 2 * OUT), F32),
            jax.ShapeDtypeStruct((N_DP, 2 * OWN + OWN // 2, 128), BF16),
        ],
        scratch_shapes=[pltpu.VMEM((BLOCK + FEATURES, EMB), F32)],
        compiler_params=room(8),
        name="towers",
    )(parts, counts, layer0, head0, layer1, head1)


def softmax_kernel(
    place_ref, group_ref, counts_ref, pooled_ref, pre_ref, hidden_ref, unit_ref, scale_ref,
    head0_ref, head1_ref, losses_ref, send_ref,
):
    size = N_DP * OWN
    group = group_ref[...]
    users = group[:, :OWN].reshape(size, OUT)
    items = group[:, OWN : 2 * OWN].reshape(size, OUT)
    counts = group[:, 2 * OWN :].astype(F32)
    counts = [jnp.concatenate([half, half], axis=2) for half in (counts[:, :, :64], counts[:, :, 64:])]
    log_freq = jnp.log(jnp.concatenate(counts, axis=1).reshape(size, 128))
    log_row = jnp.transpose(log_freq)[:1]
    own_log = jnp.log(column_of(counts_ref[...].astype(F32)))
    own_user = unit_ref[:, :OUT].astype(BF16)
    own_item = unit_ref[:, OUT:].astype(BF16)
    first = place_ref[1] * OWN
    mine = lax.broadcasted_iota(jnp.int32, (OWN, size), 1) == (
        lax.broadcasted_iota(jnp.int32, (OWN, size), 0) + first
    )
    down = INVERSE_TEMP * dot(items, users, NT) - jnp.concatenate([log_freq, log_freq], axis=1)
    lse_row = jnp.log(jnp.sum(jnp.exp(down), axis=0, keepdims=True))
    scores = INVERSE_TEMP * dot(own_user, items, NT) - log_row
    lse = jnp.log(jnp.sum(jnp.exp(scores), axis=1, keepdims=True))
    positive = jnp.sum(jnp.where(mine, scores, 0.0), axis=1, keepdims=True)
    losses_ref[...] = row_of(lse - positive)
    hot = mine.astype(F32)
    d_user = INVERSE_TEMP * dot((jnp.exp(scores - lse) - hot).astype(BF16), items)
    own_down = INVERSE_TEMP * dot(own_item, users, NT) - own_log
    d_item = INVERSE_TEMP * dot((jnp.exp(own_down - lse_row) - hot).astype(BF16), users)
    common = []
    outputs = []
    for tower, (d_unit, head_ref) in enumerate(((d_user, head0_ref), (d_item, head1_ref))):
        unit = unit_ref[:, tower * OUT : (tower + 1) * OUT]
        scale = scale_ref[:, tower * OUT : (tower + 1) * OUT]
        along = jnp.sum(unit * d_unit, axis=-1, keepdims=True)
        d_output = ((d_unit - unit * along) * scale).astype(BF16)
        pre = pre_ref[:, tower * HID : (tower + 1) * HID]
        gate = 1.0 / (1.0 + jnp.exp(-pre))
        slope = gate * (1.0 + pre * (1.0 - gate))
        common.append((dot(d_output, head_ref[...], NT) * slope).astype(BF16))
        outputs.append(d_output)
    common = jnp.concatenate(common + outputs, axis=1)
    pooled = pooled_ref[...]
    hidden = hidden_ref[...]
    blank = jnp.zeros((OWN, 64), BF16)
    for chip in range(N_CHIP):
        send_ref[chip, :, :COLUMNS_AT] = common
        send_ref[chip, :, COLUMNS_AT:] = jnp.concatenate(
            [
                pooled[:, chip * 64 : chip * 64 + 64],
                pooled[:, IN_WIDTH + chip * 64 : IN_WIDTH + chip * 64 + 64],
                hidden[:, chip * 32 : chip * 32 + 32],
                hidden[:, HID + chip * 32 : HID + chip * 32 + 32],
                blank,
            ],
            axis=1,
        )


def softmax_back(place, group, counts, pooled, pre, hidden, unit, scale, head0, head1):
    return pl.pallas_call(
        softmax_kernel,
        in_specs=[pl.BlockSpec(memory_space=pltpu.SMEM)] + [whole()] * 9,
        out_specs=[whole()] * 2,
        out_shape=[
            jax.ShapeDtypeStruct((1, OWN), F32),
            jax.ShapeDtypeStruct((N_CHIP, OWN, GRAD_WIDTH), BF16),
        ],
        compiler_params=room(6),
        name="softmax_back",
    )(place, group, counts, pooled, pre, hidden, unit, scale, head0, head1)


def back_kernel(first, *refs):
    place_ref, grads_ref, here_ref, there_ref, layer0_ref, layer1_ref = refs[:6]
    if first:
        total_ref, layers_ref, heads_ref, pooled_ref = refs[6:]
    else:
        before_ref, layers_before_ref, heads_before_ref = refs[6:9]
        send_ref, pooled_ref, layers_ref, heads_ref = refs[9:]
    samples = N_CHIP * OWN
    half = samples * FEATURES // 2
    rows = half // BACK_PARTS
    grads = grads_ref[...].reshape(samples, GRAD_WIDTH)
    inputs = grads[:, COLUMNS_AT : COLUMNS_AT + 128]
    hidden = grads[:, COLUMNS_AT + 128 :]
    d_hidden = (grads[:, :HID], grads[:, HID : 2 * HID])
    for f in range(FEATURES):
        tower = f // TOWER_FEATURES
        layer_ref = (layer0_ref, layer1_ref)[tower]
        at = (f % TOWER_FEATURES) * EMB
        pooled_ref[pl.ds(f, samples, stride=FEATURES), :] = dot(
            d_hidden[tower], layer_ref[at : at + EMB, :], NT
        )
    for tower in range(2):
        d_output = grads[:, 2 * HID + tower * OUT : 2 * HID + (tower + 1) * OUT]
        layer_rows = dot(inputs, d_hidden[tower], TN)[tower * 64 : tower * 64 + 64]
        head_rows = dot(hidden, d_output, TN)[tower * 32 : tower * 32 + 32]
        if not first:
            layer_rows = layer_rows + layers_before_ref[tower]
            head_rows = head_rows + heads_before_ref[tower]
        layers_ref[tower] = layer_rows
        heads_ref[tower] = head_rows
    total = None if first else before_ref[...]
    for other_x, weights_ref in enumerate((here_ref, there_ref)):
        first_row = (place_ref[2] ^ other_x) * half
        for part in range(BACK_PARTS):
            at = pl.ds(pl.multiple_of(first_row + part * rows, rows), rows)
            weights = weights_ref[part * rows : (part + 1) * rows, :]
            term = dot(pooled_ref[at, :].astype(BF16), weights, TN)
            total = term if total is None else total + term
    if first:
        total_ref[...] = total
        return
    table_rows = jnp.transpose(total)
    core = place_ref[0]
    for d in range(N_DP):
        send_ref[d, :64, :] = table_rows[d * 64 : (d + 1) * 64].astype(BF16)
        tower, quarter, half = d // 8, d % 8 // 2, d % 2
        send_ref[d, 64:80, :] = layers_ref[
            tower,
            pl.ds(pl.multiple_of(core * 32 + half * 16, 16), 16),
            quarter * 128 : quarter * 128 + 128,
        ].astype(BF16)
        if d < 4:
            at = pl.multiple_of(core * 16 + d % 2 * 8, 8)
            send_ref[d, 80:, :] = heads_ref[d // 2, pl.ds(at, 8), :].astype(BF16)
        else:
            send_ref[d, 80:, :] = jnp.zeros((8, 128), BF16)


def back(place, grads, weights, layer0, layer1, before=None):
    first = before is None
    total = jax.ShapeDtypeStruct((EMB, ROWS), F32)
    layers = jax.ShapeDtypeStruct((2, 64, HID), F32)
    heads = jax.ShapeDtypeStruct((2, 32, OUT), F32)
    scratch = [pltpu.VMEM((N_CHIP * BLOCK + FEATURES, EMB), F32)]
    if first:
        out_shape = [total, layers, heads]
    else:
        out_shape = [jax.ShapeDtypeStruct((N_DP, CHUNK, 128), BF16)]
        scratch += [pltpu.VMEM(layers.shape, F32), pltpu.VMEM(heads.shape, F32)]
    before = before or ()
    return pl.pallas_call(
        lambda *refs: back_kernel(first, *refs),
        in_specs=[
            pl.BlockSpec(memory_space=pltpu.SMEM),
        ]
        + [whole()] * (5 + len(before)),
        out_specs=[whole()] * len(out_shape),
        out_shape=out_shape,
        scratch_shapes=scratch,
        compiler_params=room(12),
        cost_estimate=pl.CostEstimate(
            flops=2 * N_CHIP * BLOCK * ROWS * EMB, bytes_accessed=10 * 2**20, transcendentals=0
        ),
        name="back",
    )(place, grads, *weights, layer0, layer1, *before)


def sum_kernel(parts_ref, send_ref):
    total = parts_ref[0].astype(F32)
    for d in range(1, N_DP):
        total = total + parts_ref[d].astype(F32)
    total = total.astype(BF16)
    for d in range(N_DP):
        send_ref[d] = total


def sum_parts(parts):
    return pl.pallas_call(
        sum_kernel,
        in_specs=[whole()],
        out_specs=whole(),
        out_shape=jax.ShapeDtypeStruct(parts.shape, BF16),
        compiler_params=room(2),
        name="sum_parts",
    )(parts)


def spread_kernel(sums_ref, table_ref, layer0_ref, head0_ref, layer1_ref, head1_ref):
    for d in range(N_DP):
        table_ref[d * 64 : (d + 1) * 64, :] = sums_ref[d, :64, :].astype(F32)
        tower, quarter, half = d // 8, d % 8 // 2, d % 2
        (layer0_ref, layer1_ref)[tower][
            half * 16 : half * 16 + 16, quarter * 128 : quarter * 128 + 128
        ] = sums_ref[d, 64:80, :].astype(F32)
    for d in range(4):
        (head0_ref, head1_ref)[d // 2][d % 2 * 8 : d % 2 * 8 + 8, :] = sums_ref[d, 80:, :].astype(F32)


def spread(sums):
    return pl.pallas_call(
        spread_kernel,
        in_specs=[whole()],
        out_specs=[whole()] * 5,
        out_shape=[
            jax.ShapeDtypeStruct((ROWS, EMB), F32),
            jax.ShapeDtypeStruct((32, HID), F32),
            jax.ShapeDtypeStruct((16, OUT), F32),
            jax.ShapeDtypeStruct((32, HID), F32),
            jax.ShapeDtypeStruct((16, OUT), F32),
        ],
        compiler_params=room(4),
        name="spread",
    )(sums)


def exchange(values, axes):
    return lax.all_to_all(values, axes, 0, 0, tiled=True)


def to_other(values, axis):
    return lax.ppermute(values, axis, [(0, 1), (1, 0)])


def add(*terms):
    return sum(term.astype(F32) for term in terms).astype(BF16)


def shards(ids, mults, table, user_layer, user_head, item_layer, item_head, counts):
    place = jnp.stack([lax.axis_index("core"), lax.axis_index(DP), lax.axis_index("x_lo")])
    lookups = ids[0] + 1024 * mults[0]
    both_weights, both_partial = pool(1, 1, place, lookups, table)
    both_arrived = to_other(both_partial, "core")
    x_weights, x_partial = pool(1, 0, place, lookups, table)
    x_sum, lookups = lax.optimization_barrier((add(x_partial, both_arrived), lookups))
    x_arrived = to_other(x_sum, "x_lo")
    core_weights, core_partial = pool(0, 1, place, lookups, table)
    core_arrived = to_other(core_partial, "core")
    own_weights, own_partial = pool(0, 0, place, lookups, table)
    total_partial = add(own_partial, core_arrived, x_arrived)
    parts = exchange(total_partial.reshape(N_Z, BLOCK, EMB), "z")
    pooled, pre, hidden, unit, scale, units = towers(
        parts, counts, user_layer, user_head, item_layer, item_head
    )
    group = exchange(units, DP)
    losses, grads = softmax_back(
        place, group, counts, pooled, pre, hidden, unit, scale, user_head, item_head
    )
    own_grads = exchange(grads, CHIPS)
    other_grads = to_other(own_grads, "core")
    before = back(place, own_grads, (own_weights, x_weights), user_layer, item_layer)
    (terms,) = back(
        place, other_grads, (core_weights, both_weights), user_layer, item_layer, tuple(before)
    )
    sums = exchange(sum_parts(exchange(terms, DP)), DP)
    table_change, layer0, head0, layer1, head1 = spread(sums)
    return (losses, table_change, layer0, head0, layer1, head1)


def solution(mesh):
    fine = Mesh(mesh.devices.reshape(tuple(AXES.values())), tuple(AXES))
    in_specs = (
        P(TABLE, DP, None),
        P(TABLE, DP, None),
        P(TABLE, None),
        P(),
        P(),
        P(),
        P(),
        P(DP, TABLE),
    )
    out_specs = (P(DP, TABLE),) + (P(TABLE, None),) * 5
    return jax.shard_map(shards, mesh=fine, in_specs=in_specs, out_specs=out_specs, check_vma=False)
```
